32 devices in a mesh: tok: 16 (over z, x, core), mem: 2 (over y).
Axes of the slice: x: 2, y: 2, z: 4, core: 2. Of those that a mesh axis runs over, the one named last changes fastest.
Arguments:
- queries: bfloat16 [8192, 1024], P('tok', 'mem'), may hold values from -6 to 6
- keys: bfloat16 [8192, 1024], P('tok', 'mem'), may hold values from -6 to 6
- values: bfloat16 [8192, 1024], P('tok', 'mem'), may hold values from -6 to 6
- step_sizes: float32 [4, 8192], P(None, 'tok'), may hold values from 0.05 to 0.5
- fast_weights: float32 [4, 256, 768], P(None, 'mem'), may hold values from -0.375 to 0.375
- view_lengths: int32 [32], replicated, may hold values from 1 to 512, 8192 in all
Outputs:
- layer_out: bfloat16 [8192, 1024], P('tok', 'mem')
The draws below stay inside these ranges and needn't reach their ends.
Inputs may be any that keep to these rules, and one draw needn't show every extreme that they name: `view_lengths`: the lengths sum to 8192 and the longest view has exactly 512 tokens.
All inputs are finite; a program needn't handle non-finite values.
Results may differ from the reference program's by a relative error of at most 0.011.
Values may be sent and summed in bfloat16 or wider, within the bound.
No kernel may reach another device: no remote copies, remote signals or barrier semaphores. Data moves between devices by JAX's collectives and lax.ppermute only.
A program may use at most 64 MiB of HBM per device.

```python
import math
import jax
import jax.numpy as jnp
import numpy as np
from jax import lax

NM = 4
DM = 256
FH = 256
HD = 128
TOK_DEV = 512
D = 1024
HEADS = 8
TOKENS = 8192
VIEWS = 32
N_TOK = 16


def plant_pair(base_key):
    mixed_key = jax.random.fold_in(base_key, 91)
    key_q, key_k = jax.random.split(mixed_key, 2)
    query_draw = jnp.clip(jax.random.normal(key_q, (TOKENS, D), jnp.float32), -6.0, 6.0)
    key_draw = jnp.clip(jax.random.normal(key_k, (TOKENS, D), jnp.float32), -6.0, 6.0)
    return (query_draw, key_draw)


def draw_queries(key, part):
    return plant_pair(key)[0].astype(jnp.bfloat16)


def draw_keys(key, part):
    return plant_pair(key)[1].astype(jnp.bfloat16)


def levels(stream_key, shape, cuts, low, high):
    def one(position, shards_of):
        steps = jax.random.uniform(jax.random.fold_in(jax.random.fold_in(stream_key, 6), position), (shards_of,), jnp.float32, low / len(cuts), high / len(cuts))
        return jnp.repeat(jnp.exp(steps), shape[position] // shards_of).reshape((-1,) + (1,) * (len(shape) - position - 1))

    level = one(*cuts[0])
    for cut in cuts[1:]:
        level = level * one(*cut)
    return level


def profile(number_of, total, reach, lean):
    weights = [(1 << 20) // math.isqrt(grade ** lean) + 1 for grade in range(2, number_of + 1)]
    spare, given = total - reach - (number_of - 1), [1] * (number_of - 1)
    while spare > 0:
        candidates = [i for i in range(number_of - 1) if given[i] < reach]
        pool, remaining = sum([weights[i] for i in candidates]), spare
        for i in candidates:
            extra = min(reach - given[i], max(1, remaining * weights[i] // pool), spare)
            given[i] = given[i] + extra
            spare = spare - extra
    return np.array([reach] + given)


def ragged(rng, number_of, total, limit, lean):
    if number_of == 2:
        one = jax.random.randint(rng, (), max(1, total - limit), min(limit, total - 1) + 1)
        return jnp.stack([one, total - one])
    lengths = jnp.asarray(profile(number_of, total, limit, lean), jnp.int32)
    twos = (number_of - 1) // 2
    source_of, receiver = lengths[1:1 + 2 * twos:2], lengths[2:2 + 2 * twos:2]
    room = jnp.minimum(source_of - 1, limit - receiver)
    passed = jax.random.randint(jax.random.fold_in(rng, 1), (twos,), 0, 1 << 20) % (room + 1)
    lengths = lengths.at[1:1 + 2 * twos:2].set(source_of - passed).at[2:2 + 2 * twos:2].set(receiver + passed)
    return lengths[jax.random.permutation(jax.random.fold_in(rng, 2), number_of)]


def centred(stream_key, dims, deviation, bound, cuts=(), kind=jnp.bfloat16):
    array = jax.random.normal(stream_key, dims, jnp.float32) * deviation
    if len(cuts) > 0:
        array = levels(stream_key, dims, cuts, -0.22, 0.18) * array
    return jnp.clip(array, min=-bound, max=bound).astype(kind)


def setup_inputs(seed: int = 0) -> dict:
    seeds = jax.random.split(jax.random.key(seed), 7)
    queries = draw_queries(jax.random.fold_in(seeds[6], 71), 0)
    keys = draw_keys(jax.random.fold_in(seeds[6], 71), 0)
    values = centred(seeds[2], (TOKENS, D), 1.0, 6.0, ((0, 16), (1, 2)))
    step_sizes = jnp.clip(jnp.exp(math.log(0.5) - 2.3025851 * jax.random.uniform(seeds[3], (NM, TOKENS), jnp.float32) ** levels(seeds[3], (NM, TOKENS), ((1, 16),), -0.2, 0.2)), 0.05, 0.5)
    fast_weights = centred(seeds[4], (NM, FH, 3 * DM), DM ** -0.5, 0.375, ((1, 2),), jnp.float32)
    view_lengths = ragged(seeds[5], VIEWS, TOKENS, TOK_DEV, 2).astype(jnp.int32)
    return {"queries": queries, "keys": keys, "values": values, "step_sizes": step_sizes, "fast_weights": fast_weights, "view_lengths": view_lengths}


norm_epsilon = 1e-06

def silu_pair(pre_act):
    sigmoid_val = jax.nn.sigmoid(pre_act)
    return (pre_act * sigmoid_val, sigmoid_val * (1.0 + pre_act * (1.0 - sigmoid_val)))

def renormed(weights, gradient, step_rate):
    stepped = weights - gradient * step_rate
    shaped = stepped.reshape(stepped.shape[0], 3, DM)
    before = weights.reshape(weights.shape[0], 3, DM)
    old_norm = jnp.sqrt(lax.optimization_barrier(jnp.sum(before * before, axis=2)))
    new_norm = jnp.sqrt(lax.optimization_barrier(jnp.sum(shaped * shaped, axis=2)) + norm_epsilon)
    return (shaped * (old_norm / new_norm)[:, :, None]).reshape(stepped.shape)

def memory_grads(key_part, value_part, token_rates, weights):
    rounded = weights.astype(jnp.bfloat16).astype(jnp.float32)
    weight_in = rounded[:, :DM]
    weight_up = rounded[:, DM:2 * DM]
    weight_out = rounded[:, 2 * DM:]
    key_float = key_part.astype(jnp.float32)
    gate_pre = jnp.einsum('td,fd->tf', key_float, weight_in)
    up_pre = jnp.einsum('td,fd->tf', key_float, weight_up)
    swish_val, slope_val = silu_pair(gate_pre)
    hidden = (swish_val * up_pre).astype(jnp.bfloat16).astype(jnp.float32)
    scaled = (token_rates[:, None] * value_part.astype(jnp.float32)).astype(jnp.bfloat16).astype(jnp.float32)
    grad_out = -jnp.einsum('tf,td->fd', hidden, scaled)
    back_flow = -jnp.einsum('td,fd->tf', scaled, weight_out)
    gate_back = (back_flow * up_pre * slope_val).astype(jnp.bfloat16).astype(jnp.float32)
    up_back = (back_flow * swish_val).astype(jnp.bfloat16).astype(jnp.float32)
    grad_in = jnp.einsum('tf,td->fd', gate_back, key_float)
    grad_up = jnp.einsum('tf,td->fd', up_back, key_float)
    return jnp.concatenate([grad_in, grad_up, grad_out], axis=1)

def memory_read(query_part, weights):
    rounded = weights.astype(jnp.bfloat16).astype(jnp.float32)
    query_float = query_part.astype(jnp.float32)
    gate_pre = jnp.einsum('td,fd->tf', query_float, rounded[:, :DM])
    up_pre = jnp.einsum('td,fd->tf', query_float, rounded[:, DM:2 * DM])
    swish_val, slope_val = silu_pair(gate_pre)
    read_hidden = (swish_val * up_pre).astype(jnp.bfloat16).astype(jnp.float32)
    return jnp.einsum('tf,fd->td', read_hidden, rounded[:, 2 * DM:])

def reference(queries, keys, values, step_sizes, fast_weights, view_lengths):
    view_ids = jnp.repeat(jnp.arange(VIEWS, dtype=jnp.int32), view_lengths, total_repeat_length=TOKENS).astype(jnp.int32)
    edge_fill = jnp.full((TOK_DEV,), -1, jnp.int32)
    padded_views = jnp.concatenate([edge_fill, view_ids, edge_fill])
    zero_rows = jnp.zeros((TOK_DEV, D), keys.dtype)
    padded_keys = jnp.concatenate([zero_rows, keys, zero_rows], axis=0)
    padded_values = jnp.concatenate([zero_rows, values, zero_rows], axis=0)
    score_scale = 1.0 / math.sqrt(HD)

    def one_block(block_index):
        row_start = (block_index * TOK_DEV).astype(jnp.int32)
        query_block = lax.dynamic_slice_in_dim(queries, row_start, TOK_DEV, 0).astype(jnp.float32).reshape(TOK_DEV, HEADS, HD)
        key_block = lax.dynamic_slice_in_dim(padded_keys, row_start, 3 * TOK_DEV, 0).astype(jnp.float32).reshape(3 * TOK_DEV, HEADS, HD)
        value_block = lax.dynamic_slice_in_dim(padded_values, row_start, 3 * TOK_DEV, 0).astype(jnp.float32).reshape(3 * TOK_DEV, HEADS, HD)
        query_views = lax.dynamic_slice_in_dim(view_ids, row_start, TOK_DEV, 0)
        key_views = lax.dynamic_slice_in_dim(padded_views, row_start, 3 * TOK_DEV, 0)
        scores = jnp.einsum('qhd,khd->hqk', query_block, key_block) * score_scale
        same_view = query_views[:, None] == key_views[None, :]
        scores = jnp.where(same_view[None], scores, -1e+30)
        row_peak = lax.optimization_barrier(jnp.max(scores, axis=2, keepdims=True))
        exponent = jnp.exp(scores - row_peak)
        probs = (exponent / lax.optimization_barrier(jnp.sum(exponent, axis=2, keepdims=True))).astype(jnp.bfloat16).astype(jnp.float32)
        output = jnp.einsum('hqk,khd->qhd', probs, value_block)
        return output.reshape(TOK_DEV, D)
    attended = lax.map(one_block, jnp.arange(N_TOK, dtype=jnp.int32)).reshape(TOKENS, D)
    step_rate = 1.0 / math.sqrt(TOKENS)
    pieces = []
    for memory in range(NM):
        first = memory * DM
        gradient = memory_grads(keys[:, first:first + DM], values[:, first:first + DM], step_sizes[memory], fast_weights[memory])
        updated = renormed(fast_weights[memory], gradient, step_rate)
        pieces.append(memory_read(queries[:, first:first + DM], updated))
    return (attended + jnp.concatenate(pieces, axis=1)).astype(jnp.bfloat16)
```

```python
import functools
import math

import jax
import jax.numpy as jnp
from jax import lax
from jax.experimental import pallas as pl
from jax.experimental.pallas import tpu as pltpu
from jax.sharding import PartitionSpec as P

DM = 256
HD = 128
CORES = 2
NORM_EPS = 1e-06
VMEM_BYTES = 40 * 2**20
MASKED = -1e30

BF16 = jnp.bfloat16
F32 = jnp.float32


def in_vmem(count):
    return [pl.BlockSpec(memory_space=pltpu.VMEM)] * count


def in_smem():
    return pl.BlockSpec(memory_space=pltpu.SMEM)


def params():
    return pltpu.CompilerParams(vmem_limit_bytes=VMEM_BYTES)


def dot_nt(a, b):
    return lax.dot_general(a, b, (((1,), (1,)), ((), ())), preferred_element_type=F32)


def dot_tn(a, b):
    return lax.dot_general(a, b, (((0,), (0,)), ((), ())), preferred_element_type=F32)


def dot_nn(a, b):
    return jnp.dot(a, b, preferred_element_type=F32)


def chip_digits(chips):
    digits = []
    while chips % 4 == 0:
        digits.append(4)
        chips //= 4
    if chips > 1:
        digits.append(chips)
    return digits[::-1]


def pick_kernel(chips, spots, weights_ref, rounded_ref, owned_ref):
    base, chip = spots[0], spots[1]
    memories, hidden, _ = rounded_ref.shape
    rows = hidden // chips
    for memory in range(memories):
        for block in range(chips):
            start = pl.multiple_of((chip ^ block) * rows, rows)
            part = weights_ref[base + memory, pl.ds(start, rows), :]
            rounded_ref[memory, pl.ds(block * rows, rows), :] = part.astype(BF16)
            if block == 0:
                owned_ref[memory] = part


def pick_weights(spots, weights, memories, chips):
    hidden = weights.shape[1]
    rows = hidden // chips
    shapes = (
        jax.ShapeDtypeStruct((memories, hidden, 3 * DM), BF16),
        jax.ShapeDtypeStruct((memories, rows, 3 * DM), F32),
    )
    if rows % 16:
        part = lax.dynamic_slice_in_dim(weights, spots[0], memories, 0)
        part = part.reshape(memories, chips, rows, 3 * DM)
        part = jnp.take(part, jnp.arange(chips, dtype=jnp.int32) ^ spots[1], axis=1)
        return part.reshape(shapes[0].shape).astype(BF16), part[:, 0]
    return pl.pallas_call(
        functools.partial(pick_kernel, chips),
        out_shape=shapes,
        in_specs=[in_smem()] + in_vmem(1),
        out_specs=tuple(in_vmem(2)),
        compiler_params=params(),
    )(spots, weights)


def grads_kernel(spots, own_k, own_v, mate_kv, own_rate, mate_rate, local_w, sent_w, grad_ref):
    core = spots[2]
    tokens = own_k.shape[0]
    memories, hidden, _ = local_w.shape
    for memory in range(memories):
        features = pl.ds(memory * DM, DM)
        weights = jnp.where(core == 0, local_w[memory], sent_w[memory])
        gate_up_w = jnp.concatenate([weights[:, :DM], weights[:, DM : 2 * DM]], axis=0)
        out_w = weights[:, 2 * DM :]
        grad_pair = jnp.zeros((2 * hidden, DM), F32)
        grad_out = jnp.zeros((hidden, DM), F32)
        for side in range(2):
            if side == 0:
                key, value, rate = own_k[:, features], own_v[:, features], own_rate
            else:
                key = mate_kv[pl.ds(0, tokens), features]
                value = mate_kv[pl.ds(tokens, tokens), features]
                rate = mate_rate
            rates = jnp.transpose(rate[...])[:, memory : memory + 1]
            scaled = (rates * value.astype(F32)).astype(BF16)
            gate_up = dot_nt(key, gate_up_w)
            gate, up = gate_up[:, :hidden], gate_up[:, hidden:]
            sigmoid = jax.nn.sigmoid(gate)
            swish = gate * sigmoid
            slope = sigmoid * (1.0 + gate * (1.0 - sigmoid))
            back = -dot_nt(scaled, out_w)
            pair = jnp.concatenate(
                [(back * up * slope).astype(BF16), (back * swish).astype(BF16)], axis=1
            )
            grad_pair += dot_tn(pair, key)
            grad_out -= dot_tn((swish * up).astype(BF16), scaled)
        grad_ref[memory, :, :DM] = grad_pair[:hidden].astype(BF16)
        grad_ref[memory, :, DM : 2 * DM] = grad_pair[hidden:].astype(BF16)
        grad_ref[memory, :, 2 * DM :] = grad_out.astype(BF16)


def half_grads(spots, own_k, own_v, mate_kv, own_rate, mate_rate, local_w, sent_w):
    return pl.pallas_call(
        grads_kernel,
        out_shape=jax.ShapeDtypeStruct(local_w.shape, BF16),
        in_specs=[in_smem()] + in_vmem(7),
        out_specs=in_vmem(1)[0],
        compiler_params=params(),
    )(spots, own_k, own_v, mate_kv, own_rate, mate_rate, local_w, sent_w)


def update_kernel(step_rate, parts, spots, *refs):
    grads, local_w, sent_w, new_ref = refs[:parts], refs[parts], refs[parts + 1], refs[parts + 2]
    total = grads[0][...].astype(F32)
    for part in grads[1:]:
        total += part[...].astype(F32)
    before = jnp.where(spots[2] == 0, local_w[...], sent_w[...])
    stepped = before - total * step_rate
    for block in range(3):
        columns = slice(block * DM, (block + 1) * DM)
        old, new = before[..., columns], stepped[..., columns]
        old_norm = jnp.sqrt(jnp.sum(old * old, axis=-1, keepdims=True))
        new_norm = jnp.sqrt(jnp.sum(new * new, axis=-1, keepdims=True) + NORM_EPS)
        new_ref[:, :, columns] = (new * (old_norm / new_norm)).astype(BF16)


def update_rows(spots, step_rate, grads, local_w, sent_w):
    return pl.pallas_call(
        functools.partial(update_kernel, step_rate, len(grads)),
        out_shape=jax.ShapeDtypeStruct(local_w.shape, BF16),
        in_specs=[in_smem()] + in_vmem(len(grads) + 2),
        out_specs=in_vmem(1)[0],
        compiler_params=params(),
    )(spots, *grads, local_w, sent_w)


def attend_kernel(spots, lengths, q_ref, own_k, own_v, mate_kv, far_kv, out_ref):
    tokens, width = q_ref.shape
    views = lengths.shape[0]
    own = spots[3]
    bases = (own, spots[4], spots[5])
    upto = lax.broadcasted_iota(jnp.int32, (views, views), 0) <= lax.broadcasted_iota(
        jnp.int32, (views, views), 1
    )
    ends = jnp.sum(jnp.where(upto, lengths[...], 0), axis=0, keepdims=True)
    spot = own + lax.broadcasted_iota(jnp.int32, (tokens, 1), 0)
    stop = jnp.min(jnp.where(ends > spot, ends, jnp.int32(2**30)), axis=1, keepdims=True)
    start = jnp.max(jnp.where(ends <= spot, ends, 0), axis=1, keepdims=True)
    scale = math.log2(math.e) / math.sqrt(HD)
    block_rows = tokens // 2
    for block in range(2):
        rows = pl.ds(block * block_rows, block_rows)
        first = start[block * block_rows : (block + 1) * block_rows]
        last = stop[block * block_rows : (block + 1) * block_rows]
        masks = []
        for base in bases:
            place = base + lax.broadcasted_iota(jnp.int32, (1, tokens), 1)
            masks.append((place >= first) & (place < last))
        for head in range(width // HD):
            lanes = pl.ds(head * HD, HD)
            query = q_ref[rows, lanes]
            key_parts = (own_k[:, lanes], mate_kv[:tokens, lanes], far_kv[:tokens, lanes])
            scores = [
                jnp.where(mask, dot_nt(query, key) * scale, MASKED)
                for mask, key in zip(masks, key_parts)
            ]
            peak = functools.reduce(
                jnp.maximum, [jnp.max(s, axis=1, keepdims=True) for s in scores]
            )
            weights = [jnp.exp2(s - peak) for s in scores]
            total = sum(jnp.sum(w, axis=1, keepdims=True) for w in weights)
            value_parts = (own_v[:, lanes], mate_kv[tokens:, lanes], far_kv[tokens:, lanes])
            mixed = sum(dot_nn(w.astype(BF16), v) for w, v in zip(weights, value_parts))
            out_ref[rows, lanes] = mixed / total


def attend(spots, lengths, queries, keys, values, mate_kv, far_kv):
    return pl.pallas_call(
        attend_kernel,
        out_shape=jax.ShapeDtypeStruct(queries.shape, F32),
        in_specs=[in_smem()] + in_vmem(6),
        out_specs=in_vmem(1)[0],
        compiler_params=params(),
    )(spots, lengths, queries, keys, values, mate_kv, far_kv)


def read_kernel(q_ref, own_w, mate_w, attended_ref, out_ref):
    chips, memories, rows, _ = own_w.shape
    for memory in range(memories):
        features = pl.ds(memory * DM, DM)
        query = q_ref[:, features]
        total = attended_ref[:, features]
        for half in (own_w, mate_w):
            weights = half[:, memory].reshape(chips * rows, 3 * DM)
            gate = dot_nt(query, weights[:, :DM])
            up = dot_nt(query, weights[:, DM : 2 * DM])
            hidden = (gate * jax.nn.sigmoid(gate) * up).astype(BF16)
            total += dot_nn(hidden, weights[:, 2 * DM :])
        out_ref[:, features] = total.astype(BF16)


def read_out(queries, own_w, mate_w, attended):
    return pl.pallas_call(
        read_kernel,
        out_shape=jax.ShapeDtypeStruct(queries.shape, BF16),
        in_specs=in_vmem(4),
        out_specs=in_vmem(1)[0],
        compiler_params=params(),
    )(queries, own_w, mate_w, attended)


def on_device(queries, keys, values, step_sizes, fast_weights, view_lengths):
    tokens = queries.shape[0]
    memories = queries.shape[1] // DM
    devices = lax.axis_size("tok")
    planes = lax.axis_size("mem")
    chips = devices // CORES
    digits = chip_digits(chips)
    spot, plane = lax.axis_index("tok"), lax.axis_index("mem")
    core, chip = spot % CORES, spot // CORES
    mate = spot ^ 1
    far = jnp.where(core == 0, spot - 1, spot + 1)
    source = jnp.where(core == 0, plane, planes - 1 - plane) * memories
    spots = jnp.stack([source, chip, core, spot * tokens, mate * tokens, far * tokens]).astype(
        jnp.int32
    )

    def to_core(x):
        return lax.ppermute(x, "tok", [(i, i ^ 1) for i in range(devices)])

    def to_far(x):
        pairs = [(i, i + 1) for i in range(1, devices - 1, 2)]
        pairs += [(i + 1, i) for i in range(1, devices - 1, 2)]
        return lax.ppermute(x, "tok", pairs)

    def to_chip(x, flip):
        pairs = [(i, (((i // CORES) ^ flip) * CORES) + i % CORES) for i in range(devices)]
        return lax.ppermute(x, "tok", pairs)

    def to_plane(x):
        pairs = [
            (i * planes + p, i * planes + planes - 1 - p)
            for i in range(1, devices, CORES)
            for p in range(planes)
        ]
        return lax.ppermute(x, ("tok", "mem"), pairs)

    local_w, local_rows = pick_weights(spots, fast_weights, memories, chips)
    sent_w = to_plane(local_w)
    pair = jnp.concatenate([keys, values], axis=0)
    mate_kv = to_core(pair)
    far_kv = to_far(pair)
    rates = lax.dynamic_slice_in_dim(step_sizes, plane * memories, memories, 0)
    rates = jnp.pad(rates, ((0, -memories % 8), (0, 0)))
    mate_rates = to_core(rates)
    sent_rows = to_plane(local_rows)

    grads = half_grads(spots, keys, values, mate_kv, rates, mate_rates, local_w, sent_w)
    rows = grads.shape[1] // chips
    held = grads.reshape(memories, chips, rows, 3 * DM).transpose(1, 0, 2, 3)
    stride = 1
    for place, radix in enumerate(digits):
        held = held.reshape((held.shape[0] // radix, radix) + held.shape[1:])
        kept = held[:, 0]
        came = [to_chip(held[:, step], step * stride) for step in range(1, radix)]
        stride *= radix
        if place < len(digits) - 1:
            held = sum([part.astype(F32) for part in came], kept.astype(F32)).astype(BF16)
    parts = [part.reshape(memories, rows, 3 * DM) for part in [kept] + came]
    all_tokens = tokens * devices
    fresh = update_rows(spots, 1.0 / math.sqrt(all_tokens), parts, local_rows, sent_rows)

    gathered = fresh[None]
    stride = 1
    for radix in digits:
        came = [to_chip(gathered, step * stride) for step in range(1, radix)]
        gathered = jnp.concatenate([gathered] + came, axis=0)
        stride *= radix
    mate_w = to_core(gathered)

    attended = attend(
        spots, view_lengths.reshape(-1, 1), queries, keys, values, mate_kv, far_kv
    )
    return read_out(queries, gathered, mate_w, attended)


def solution(mesh):
    placed = (
        P("tok", "mem"),
        P("tok", "mem"),
        P("tok", "mem"),
        P(None, "tok"),
        P(None, "mem", None),
        P(),
    )
    return jax.shard_map(
        on_device, mesh=mesh, in_specs=placed, out_specs=P("tok", "mem"), check_vma=False
    )
```

```python
import functools
import math

import jax
import jax.numpy as jnp
from jax import lax
from jax.experimental import pallas as pl
from jax.experimental.pallas import tpu as pltpu
from jax.sharding import PartitionSpec as P

DM = 256
HD = 128
CORES = 2
NORM_EPS = 1e-06
VMEM_BYTES = 40 * 2**20
MASKED = -1e30

BF16 = jnp.bfloat16
F32 = jnp.float32


def in_vmem(count):
    return [pl.BlockSpec(memory_space=pltpu.VMEM)] * count


def in_smem():
    return pl.BlockSpec(memory_space=pltpu.SMEM)


def params():
    return pltpu.CompilerParams(vmem_limit_bytes=VMEM_BYTES)


def dot_nt(a, b):
    return lax.dot_general(a, b, (((1,), (1,)), ((), ())), preferred_element_type=F32)


def dot_tn(a, b):
    return lax.dot_general(a, b, (((0,), (0,)), ((), ())), preferred_element_type=F32)


def dot_nn(a, b):
    return jnp.dot(a, b, preferred_element_type=F32)


def chip_digits(chips):
    digits = []
    while chips % 4 == 0:
        digits.append(4)
        chips //= 4
    if chips > 1:
        digits.append(chips)
    return digits[::-1]


def pick_kernel(chips, spots, weights_ref, picked_ref):
    base, chip = spots[0], spots[1]
    memories, hidden = picked_ref.shape[0], weights_ref.shape[1]
    rows = hidden // chips
    for memory in range(memories):
        for block in range(chips):
            start = pl.multiple_of((chip ^ block) * rows, rows)
            part = weights_ref[base + memory, pl.ds(start, rows), :]
            rounded = part.astype(BF16)
            picked_ref[memory, pl.ds(block * rows, rows), :] = rounded
            if block == 0:
                rest = part - rounded.astype(F32)
                picked_ref[memory, pl.ds(hidden, rows), :] = rest.astype(BF16)


def pick_weights(spots, weights, memories, chips):
    hidden = weights.shape[1]
    rows = hidden // chips
    if rows % 16:
        part = lax.dynamic_slice_in_dim(weights, spots[0], memories, 0)
        part = part.reshape(memories, chips, rows, 3 * DM)
        part = jnp.take(part, jnp.arange(chips, dtype=jnp.int32) ^ spots[1], axis=1)
        rounded = part.astype(BF16)
        rest = (part[:, :1] - rounded[:, :1].astype(F32)).astype(BF16)
        picked = jnp.concatenate([rounded, rest], axis=1)
        return picked.reshape(memories, hidden + rows, 3 * DM)
    return pl.pallas_call(
        functools.partial(pick_kernel, chips),
        out_shape=jax.ShapeDtypeStruct((memories, hidden + rows, 3 * DM), BF16),
        in_specs=[in_smem()] + in_vmem(1),
        out_specs=in_vmem(1)[0],
        compiler_params=params(),
    )(spots, weights)


def grads_kernel(
    spots, own_k, own_v, mate_k, mate_v, own_rate, mate_rate, local_w, sent_w, grad_ref
):
    core = spots[2]
    memories, hidden, _ = grad_ref.shape
    for memory in range(memories):
        features = pl.ds(memory * DM, DM)
        weights = jnp.where(core == 0, local_w[memory, :hidden], sent_w[memory, :hidden])
        gate_up_w = jnp.concatenate([weights[:, :DM], weights[:, DM : 2 * DM]], axis=0)
        out_w = weights[:, 2 * DM :]
        grad_pair = jnp.zeros((2 * hidden, DM), F32)
        grad_out = jnp.zeros((hidden, DM), F32)
        for key_ref, value_ref, rate in ((own_k, own_v, own_rate), (mate_k, mate_v, mate_rate)):
            key, value = key_ref[:, features], value_ref[:, features]
            rates = jnp.transpose(rate[...])[:, memory : memory + 1]
            scaled = (rates * value.astype(F32)).astype(BF16)
            gate_up = dot_nt(key, gate_up_w)
            gate, up = gate_up[:, :hidden], gate_up[:, hidden:]
            sigmoid = jax.nn.sigmoid(gate)
            swish = gate * sigmoid
            slope = sigmoid * (1.0 + gate * (1.0 - sigmoid))
            back = -dot_nt(scaled, out_w)
            pair = jnp.concatenate(
                [(back * up * slope).astype(BF16), (back * swish).astype(BF16)], axis=1
            )
            grad_pair += dot_tn(pair, key)
            grad_out -= dot_tn((swish * up).astype(BF16), scaled)
        grad_ref[memory, :, :DM] = grad_pair[:hidden].astype(BF16)
        grad_ref[memory, :, DM : 2 * DM] = grad_pair[hidden:].astype(BF16)
        grad_ref[memory, :, 2 * DM :] = grad_out.astype(BF16)


def half_grads(spots, hidden, own_k, own_v, mate_k, mate_v, own_rate, mate_rate, local_w, sent_w):
    shape = (local_w.shape[0], hidden, local_w.shape[2])
    return pl.pallas_call(
        grads_kernel,
        out_shape=jax.ShapeDtypeStruct(shape, BF16),
        in_specs=[in_smem()] + in_vmem(8),
        out_specs=in_vmem(1)[0],
        compiler_params=params(),
    )(spots, own_k, own_v, mate_k, mate_v, own_rate, mate_rate, local_w, sent_w)


def update_kernel(step_rate, parts, spots, *refs):
    grads, local_w, sent_w, new_ref = refs[:parts], refs[parts], refs[parts + 1], refs[parts + 2]
    total = grads[0][...].astype(F32)
    for part in grads[1:]:
        total += part[...].astype(F32)
    rows = new_ref.shape[1]
    picked = jnp.where(spots[2] == 0, local_w[...], sent_w[...]).astype(F32)
    before = picked[:, :rows] + picked[:, -rows:]
    stepped = before - total * step_rate
    for block in range(3):
        columns = slice(block * DM, (block + 1) * DM)
        old, new = before[..., columns], stepped[..., columns]
        old_norm = jnp.sqrt(jnp.sum(old * old, axis=-1, keepdims=True))
        new_norm = jnp.sqrt(jnp.sum(new * new, axis=-1, keepdims=True) + NORM_EPS)
        new_ref[:, :, columns] = (new * (old_norm / new_norm)).astype(BF16)


def update_rows(spots, step_rate, grads, local_w, sent_w):
    return pl.pallas_call(
        functools.partial(update_kernel, step_rate, len(grads)),
        out_shape=jax.ShapeDtypeStruct(grads[0].shape, BF16),
        in_specs=[in_smem()] + in_vmem(len(grads) + 2),
        out_specs=in_vmem(1)[0],
        compiler_params=params(),
    )(spots, *grads, local_w, sent_w)


def view_bounds(lengths, own, tokens):
    views = lengths.shape[0]
    upto = lax.broadcasted_iota(jnp.int32, (views, views), 0) <= lax.broadcasted_iota(
        jnp.int32, (views, views), 1
    )
    ends = jnp.sum(jnp.where(upto, lengths[...], 0), axis=0, keepdims=True)
    spot = own + lax.broadcasted_iota(jnp.int32, (tokens, 1), 0)
    stop = jnp.min(jnp.where(ends > spot, ends, jnp.int32(2**30)), axis=1, keepdims=True)
    start = jnp.max(jnp.where(ends <= spot, ends, 0), axis=1, keepdims=True)
    return start, stop


def inside(base, count, start, stop):
    place = base + lax.broadcasted_iota(jnp.int32, (1, count), 1)
    return (place >= start) & (place < stop)


SCORE_SCALE = math.log2(math.e) / math.sqrt(HD)


def near_kernel(spots, lengths, q_ref, own_k, own_v, mate_k, mate_v, mixed_ref, peak_ref, sum_ref):
    tokens, width = q_ref.shape
    start, stop = view_bounds(lengths, spots[3], tokens)
    block_rows = tokens // 2
    for block in range(2):
        rows = slice(block * block_rows, (block + 1) * block_rows)
        masks = [inside(spots[3 + i], tokens, start[rows], stop[rows]) for i in range(2)]
        for head in range(width // HD):
            lanes = pl.ds(head * HD, HD)
            query = q_ref[rows, lanes]
            scores = [
                jnp.where(mask, dot_nt(query, key[:, lanes]) * SCORE_SCALE, MASKED)
                for mask, key in zip(masks, (own_k, mate_k))
            ]
            peak = functools.reduce(
                jnp.maximum, [jnp.max(s, axis=1, keepdims=True) for s in scores]
            )
            weights = [jnp.exp2(s - peak) for s in scores]
            peak_ref[rows, head : head + 1] = peak
            sum_ref[rows, head : head + 1] = sum(
                jnp.sum(w, axis=1, keepdims=True) for w in weights
            )
            mixed_ref[rows, lanes] = sum(
                dot_nn(w.astype(BF16), v[:, lanes]) for w, v in zip(weights, (own_v, mate_v))
            )


def far_kernel(
    spots, lengths, q_ref, far_k, far_v, mixed_ref, peak_ref, sum_ref, out_ref
):
    tokens, width = q_ref.shape
    start, stop = view_bounds(lengths, spots[3], tokens)
    block_rows = tokens // 2
    for block in range(2):
        rows = slice(block * block_rows, (block + 1) * block_rows)
        mask = inside(spots[5], tokens, start[rows], stop[rows])
        for head in range(width // HD):
            lanes = pl.ds(head * HD, HD)
            scores = dot_nt(q_ref[rows, lanes], far_k[:, lanes]) * SCORE_SCALE
            scores = jnp.where(mask, scores, MASKED)
            before = peak_ref[rows, head : head + 1]
            peak = jnp.maximum(before, jnp.max(scores, axis=1, keepdims=True))
            weights = jnp.exp2(scores - peak)
            shrink = jnp.exp2(before - peak)
            total = sum_ref[rows, head : head + 1] * shrink + jnp.sum(
                weights, axis=1, keepdims=True
            )
            mixed = mixed_ref[rows, lanes] * shrink + dot_nn(
                weights.astype(BF16), far_v[:, lanes]
            )
            out_ref[rows, lanes] = mixed / total


def attend_near(spots, lengths, queries, keys, values, mate_k, mate_v):
    tokens, width = queries.shape
    stats = jax.ShapeDtypeStruct((tokens, width // HD), F32)
    return pl.pallas_call(
        near_kernel,
        out_shape=(jax.ShapeDtypeStruct(queries.shape, F32), stats, stats),
        in_specs=[in_smem()] + in_vmem(6),
        out_specs=tuple(in_vmem(3)),
        compiler_params=params(),
    )(spots, lengths, queries, keys, values, mate_k, mate_v)


def attend_far(spots, lengths, queries, far_k, far_v, near):
    return pl.pallas_call(
        far_kernel,
        out_shape=jax.ShapeDtypeStruct(queries.shape, F32),
        in_specs=[in_smem()] + in_vmem(7),
        out_specs=in_vmem(1)[0],
        compiler_params=params(),
    )(spots, lengths, queries, far_k, far_v, *near)


def read_kernel(q_ref, own_w, mate_w, attended_ref, out_ref):
    chips, memories, rows, _ = own_w.shape
    for memory in range(memories):
        features = pl.ds(memory * DM, DM)
        query = q_ref[:, features]
        total = attended_ref[:, features]
        for half in (own_w, mate_w):
            weights = half[:, memory].reshape(chips * rows, 3 * DM)
            gate = dot_nt(query, weights[:, :DM])
            up = dot_nt(query, weights[:, DM : 2 * DM])
            hidden = (gate * jax.nn.sigmoid(gate) * up).astype(BF16)
            total += dot_nn(hidden, weights[:, 2 * DM :])
        out_ref[:, features] = total.astype(BF16)


def read_out(queries, own_w, mate_w, attended):
    return pl.pallas_call(
        read_kernel,
        out_shape=jax.ShapeDtypeStruct(queries.shape, BF16),
        in_specs=in_vmem(4),
        out_specs=in_vmem(1)[0],
        compiler_params=params(),
    )(queries, own_w, mate_w, attended)


def on_device(queries, keys, values, step_sizes, fast_weights, view_lengths):
    tokens = queries.shape[0]
    memories = queries.shape[1] // DM
    devices = lax.axis_size("tok")
    planes = lax.axis_size("mem")
    chips = devices // CORES
    digits = chip_digits(chips)
    spot, plane = lax.axis_index("tok"), lax.axis_index("mem")
    core, chip = spot % CORES, spot // CORES
    mate = spot ^ 1
    far = jnp.where(core == 0, spot - 1, spot + 1)
    source = jnp.where(core == 0, plane, planes - 1 - plane) * memories
    spots = jnp.stack([source, chip, core, spot * tokens, mate * tokens, far * tokens]).astype(
        jnp.int32
    )

    def to_core(x):
        return lax.ppermute(x, "tok", [(i, i ^ 1) for i in range(devices)])

    def to_far(x):
        pairs = [(i, i + 1) for i in range(1, devices - 1, 2)]
        pairs += [(i + 1, i) for i in range(1, devices - 1, 2)]
        return lax.ppermute(x, "tok", pairs)

    def to_chip(x, flip):
        pairs = [(i, (((i // CORES) ^ flip) * CORES) + i % CORES) for i in range(devices)]
        return lax.ppermute(x, "tok", pairs)

    def to_plane(x):
        pairs = [
            (i * planes + p, i * planes + planes - 1 - p)
            for i in range(1, devices, CORES)
            for p in range(planes)
        ]
        return lax.ppermute(x, ("tok", "mem"), pairs)

    hidden = fast_weights.shape[1]
    rows = hidden // chips
    local_w = pick_weights(spots, fast_weights, memories, chips)
    sent_w = to_plane(local_w)
    far_k = to_far(keys)
    mate_k, mate_v = to_core(keys), to_core(values)
    rates = lax.dynamic_slice_in_dim(step_sizes, plane * memories, memories, 0)
    rates = jnp.pad(rates, ((0, -memories % 8), (0, 0)))
    mate_rates = to_core(rates)
    lengths = view_lengths.reshape(-1, 1)

    near = attend_near(spots, lengths, queries, keys, values, mate_k, mate_v)
    grads = half_grads(
        spots, hidden, keys, values, mate_k, mate_v, rates, mate_rates, local_w, sent_w
    )
    grads, far_k, near = lax.optimization_barrier((grads, far_k, near))
    held = grads.reshape(memories, chips, rows, 3 * DM).transpose(1, 0, 2, 3)
    far_v = None
    stride = 1
    for place, radix in enumerate(digits):
        held = held.reshape((held.shape[0] // radix, radix) + held.shape[1:])
        kept = held[:, 0]
        came = [to_chip(held[:, step], step * stride) for step in range(1, radix)]
        if far_v is None:
            came, far_v = lax.optimization_barrier((came, values))
            far_v = to_far(far_v)
        stride *= radix
        if place < len(digits) - 1:
            held = sum([part.astype(F32) for part in came], kept.astype(F32)).astype(BF16)
    parts = [part.reshape(memories, rows, 3 * DM) for part in [kept] + came]
    all_tokens = tokens * devices
    fresh = update_rows(spots, 1.0 / math.sqrt(all_tokens), parts, local_w, sent_w)

    gathered = fresh[None]
    for place, radix in enumerate(digits[::-1]):
        stride //= radix
        if place == len(digits) - 1:
            gathered, far_v = lax.optimization_barrier((gathered, far_v))
        came = [to_chip(gathered, step * stride) for step in range(1, radix)]
        if place == len(digits) - 1:
            attended = attend_far(spots, lengths, queries, far_k, far_v, near)
            came, attended = lax.optimization_barrier((came, attended))
        gathered = jnp.concatenate([gathered] + came, axis=0)
    mate_w = to_core(gathered)

    return read_out(queries, gathered, mate_w, attended)


def solution(mesh):
    placed = (
        P("tok", "mem"),
        P("tok", "mem"),
        P("tok", "mem"),
        P(None, "tok"),
        P(None, "mem", None),
        P(),
    )
    return jax.shard_map(
        on_device, mesh=mesh, in_specs=placed, out_specs=P("tok", "mem"), check_vma=False
    )
```

```python
import functools
import math

import jax
import jax.numpy as jnp
from jax import lax
from jax.experimental import pallas as pl
from jax.experimental.pallas import tpu as pltpu
from jax.sharding import PartitionSpec as P

DM = 256
HD = 128
CORES = 2
NORM_EPS = 1e-06
VMEM_BYTES = 40 * 2**20
MASKED = -1e30

BF16 = jnp.bfloat16
F32 = jnp.float32


def in_vmem(count):
    return [pl.BlockSpec(memory_space=pltpu.VMEM)] * count


def in_smem():
    return pl.BlockSpec(memory_space=pltpu.SMEM)


def params():
    return pltpu.CompilerParams(vmem_limit_bytes=VMEM_BYTES)


def dot_nt(a, b):
    return lax.dot_general(a, b, (((1,), (1,)), ((), ())), preferred_element_type=F32)


def dot_tn(a, b):
    return lax.dot_general(a, b, (((0,), (0,)), ((), ())), preferred_element_type=F32)


def dot_nn(a, b):
    return jnp.dot(a, b, preferred_element_type=F32)


def chip_digits(chips):
    digits = []
    while chips % 4 == 0:
        digits.append(4)
        chips //= 4
    if chips > 1:
        digits.append(chips)
    return digits[::-1]


def grads_kernel(
    spots, own_k, own_v, mate_k, mate_v, own_rate, mate_rate, local_w, sent_w, grad_ref
):
    chip, core = spots[1], spots[2]
    memories, hidden, _ = local_w.shape
    for memory in range(memories):
        features = pl.ds(memory * DM, DM)
        weights = jnp.where(core == 0, local_w[memory], sent_w[memory])
        gate_up_w = jnp.concatenate([weights[:, :DM], weights[:, DM : 2 * DM]], axis=0)
        out_w = weights[:, 2 * DM :]
        grad_pair = jnp.zeros((2 * hidden, DM), F32)
        grad_out = jnp.zeros((hidden, DM), F32)
        for key_ref, value_ref, rate in ((own_k, own_v, own_rate), (mate_k, mate_v, mate_rate)):
            key, value = key_ref[:, features], value_ref[:, features]
            rates = jnp.transpose(rate[...])[:, memory : memory + 1]
            scaled = (rates * value.astype(F32)).astype(BF16)
            gate_up = dot_nt(key, gate_up_w)
            gate, up = gate_up[:, :hidden], gate_up[:, hidden:]
            sigmoid = jax.nn.sigmoid(gate)
            swish = gate * sigmoid
            slope = sigmoid * (1.0 + gate * (1.0 - sigmoid))
            back = -dot_nt(scaled, out_w)
            pair = jnp.concatenate(
                [(back * up * slope).astype(BF16), (back * swish).astype(BF16)], axis=1
            )
            grad_pair += dot_tn(pair, key)
            grad_out -= dot_tn((swish * up).astype(BF16), scaled)
        found = (grad_pair[:hidden], grad_pair[hidden:], grad_out)
        for part, grad in enumerate(found):
            grad = grad.astype(BF16)
            columns = pl.ds(part * DM, DM)
            if grad_ref.ndim == 3:
                grad_ref[memory, :, columns] = grad
            else:
                chips, _, rows, _ = grad_ref.shape
                for block in range(chips):
                    piece = grad[block * rows : (block + 1) * rows]
                    grad_ref[chip ^ block, memory, :, columns] = piece


def half_grads(spots, chips, own_k, own_v, mate_k, mate_v, own_rate, mate_rate, local_w, sent_w):
    memories, hidden, width = local_w.shape
    rows = hidden // chips
    placed = rows % 16 == 0
    shape = (chips, memories, rows, width) if placed else local_w.shape
    grads = pl.pallas_call(
        grads_kernel,
        out_shape=jax.ShapeDtypeStruct(shape, BF16),
        in_specs=[in_smem()] + in_vmem(8),
        out_specs=in_vmem(1)[0],
        compiler_params=params(),
    )(spots, own_k, own_v, mate_k, mate_v, own_rate, mate_rate, local_w, sent_w)
    if placed:
        return grads
    grads = grads.reshape(memories, chips, rows, width).transpose(1, 0, 2, 3)
    return jnp.take(grads, jnp.arange(chips, dtype=jnp.int32) ^ spots[1], axis=0)


def update_kernel(step_rate, parts, spots, *refs):
    grads, local_w, sent_w, new_ref = refs[:parts], refs[parts], refs[parts + 1], refs[parts + 2]
    total = grads[0][...].astype(F32)
    for part in grads[1:]:
        total += part[...].astype(F32)
    before = jnp.where(spots[2] == 0, local_w[...], sent_w[...])
    stepped = before - total * step_rate
    for block in range(3):
        columns = slice(block * DM, (block + 1) * DM)
        old, new = before[..., columns], stepped[..., columns]
        old_norm = jnp.sqrt(jnp.sum(old * old, axis=-1, keepdims=True))
        new_norm = jnp.sqrt(jnp.sum(new * new, axis=-1, keepdims=True) + NORM_EPS)
        new_ref[:, :, columns] = (new * (old_norm / new_norm)).astype(BF16)


def update_rows(spots, step_rate, grads, local_w, sent_w):
    return pl.pallas_call(
        functools.partial(update_kernel, step_rate, len(grads)),
        out_shape=jax.ShapeDtypeStruct(grads[0].shape, BF16),
        in_specs=[in_smem()] + in_vmem(len(grads) + 2),
        out_specs=in_vmem(1)[0],
        compiler_params=params(),
    )(spots, *grads, local_w, sent_w)


def view_bounds(lengths, own, tokens):
    views = lengths.shape[0]
    upto = lax.broadcasted_iota(jnp.int32, (views, views), 0) <= lax.broadcasted_iota(
        jnp.int32, (views, views), 1
    )
    ends = jnp.sum(jnp.where(upto, lengths[...], 0), axis=0, keepdims=True)
    spot = own + lax.broadcasted_iota(jnp.int32, (tokens, 1), 0)
    stop = jnp.min(jnp.where(ends > spot, ends, jnp.int32(2**30)), axis=1, keepdims=True)
    start = jnp.max(jnp.where(ends <= spot, ends, 0), axis=1, keepdims=True)
    return start, stop


def inside(base, count, start, stop):
    place = base + lax.broadcasted_iota(jnp.int32, (1, count), 1)
    return (place >= start) & (place < stop)


SCORE_SCALE = math.log2(math.e) / math.sqrt(HD)


def near_kernel(spots, lengths, q_ref, own_k, own_v, mate_k, mate_v, mixed_ref, peak_ref, sum_ref):
    tokens, width = q_ref.shape
    start, stop = view_bounds(lengths, spots[3], tokens)
    block_rows = tokens // 2
    for block in range(2):
        rows = slice(block * block_rows, (block + 1) * block_rows)
        masks = [inside(spots[3 + i], tokens, start[rows], stop[rows]) for i in range(2)]
        for head in range(width // HD):
            lanes = pl.ds(head * HD, HD)
            query = q_ref[rows, lanes]
            scores = [
                jnp.where(mask, dot_nt(query, key[:, lanes]) * SCORE_SCALE, MASKED)
                for mask, key in zip(masks, (own_k, mate_k))
            ]
            peak = functools.reduce(
                jnp.maximum, [jnp.max(s, axis=1, keepdims=True) for s in scores]
            )
            weights = [jnp.exp2(s - peak) for s in scores]
            peak_ref[rows, head : head + 1] = peak
            sum_ref[rows, head : head + 1] = sum(
                jnp.sum(w, axis=1, keepdims=True) for w in weights
            )
            mixed_ref[rows, lanes] = sum(
                dot_nn(w.astype(BF16), v[:, lanes]) for w, v in zip(weights, (own_v, mate_v))
            )


def far_kernel(
    spots, lengths, q_ref, far_k, far_v, mixed_ref, peak_ref, sum_ref, out_ref
):
    tokens, width = q_ref.shape
    start, stop = view_bounds(lengths, spots[3], tokens)
    block_rows = tokens // 2
    for block in range(2):
        rows = slice(block * block_rows, (block + 1) * block_rows)
        mask = inside(spots[5], tokens, start[rows], stop[rows])
        for head in range(width // HD):
            lanes = pl.ds(head * HD, HD)
            scores = dot_nt(q_ref[rows, lanes], far_k[:, lanes]) * SCORE_SCALE
            scores = jnp.where(mask, scores, MASKED)
            before = peak_ref[rows, head : head + 1]
            peak = jnp.maximum(before, jnp.max(scores, axis=1, keepdims=True))
            weights = jnp.exp2(scores - peak)
            shrink = jnp.exp2(before - peak)
            total = sum_ref[rows, head : head + 1] * shrink + jnp.sum(
                weights, axis=1, keepdims=True
            )
            mixed = mixed_ref[rows, lanes] * shrink + dot_nn(
                weights.astype(BF16), far_v[:, lanes]
            )
            out_ref[rows, lanes] = mixed / total


def attend_near(spots, lengths, queries, keys, values, mate_k, mate_v):
    tokens, width = queries.shape
    stats = jax.ShapeDtypeStruct((tokens, width // HD), F32)
    return pl.pallas_call(
        near_kernel,
        out_shape=(jax.ShapeDtypeStruct(queries.shape, F32), stats, stats),
        in_specs=[in_smem()] + in_vmem(6),
        out_specs=tuple(in_vmem(3)),
        compiler_params=params(),
    )(spots, lengths, queries, keys, values, mate_k, mate_v)


def attend_far(spots, lengths, queries, far_k, far_v, near):
    return pl.pallas_call(
        far_kernel,
        out_shape=jax.ShapeDtypeStruct(queries.shape, F32),
        in_specs=[in_smem()] + in_vmem(7),
        out_specs=in_vmem(1)[0],
        compiler_params=params(),
    )(spots, lengths, queries, far_k, far_v, *near)


def read_kernel(q_ref, own_w, mate_w, attended_ref, out_ref):
    chips, memories, rows, _ = own_w.shape
    for memory in range(memories):
        features = pl.ds(memory * DM, DM)
        query = q_ref[:, features]
        total = attended_ref[:, features]
        for half in (own_w, mate_w):
            weights = half[:, memory].reshape(chips * rows, 3 * DM)
            gate = dot_nt(query, weights[:, :DM])
            up = dot_nt(query, weights[:, DM : 2 * DM])
            hidden = (gate * jax.nn.sigmoid(gate) * up).astype(BF16)
            total += dot_nn(hidden, weights[:, 2 * DM :])
        out_ref[:, features] = total.astype(BF16)


def read_out(queries, own_w, mate_w, attended):
    return pl.pallas_call(
        read_kernel,
        out_shape=jax.ShapeDtypeStruct(queries.shape, BF16),
        in_specs=in_vmem(4),
        out_specs=in_vmem(1)[0],
        compiler_params=params(),
    )(queries, own_w, mate_w, attended)


def on_device(queries, keys, values, step_sizes, fast_weights, view_lengths):
    tokens = queries.shape[0]
    memories = queries.shape[1] // DM
    devices = lax.axis_size("tok")
    planes = lax.axis_size("mem")
    chips = devices // CORES
    digits = chip_digits(chips)
    spot, plane = lax.axis_index("tok"), lax.axis_index("mem")
    core, chip = spot % CORES, spot // CORES
    mate = spot ^ 1
    far = jnp.where(core == 0, spot - 1, spot + 1)
    source = jnp.where(core == 0, plane, planes - 1 - plane) * memories
    spots = jnp.stack([source, chip, core, spot * tokens, mate * tokens, far * tokens]).astype(
        jnp.int32
    )

    def to_core(x):
        return lax.ppermute(x, "tok", [(i, i ^ 1) for i in range(devices)])

    def to_far(x):
        pairs = [(i, i + 1) for i in range(1, devices - 1, 2)]
        pairs += [(i + 1, i) for i in range(1, devices - 1, 2)]
        return lax.ppermute(x, "tok", pairs)

    def to_chip(x, flip):
        pairs = [(i, (((i // CORES) ^ flip) * CORES) + i % CORES) for i in range(devices)]
        return lax.ppermute(x, "tok", pairs)

    def to_plane(x):
        pairs = [
            (i * planes + p, i * planes + planes - 1 - p)
            for i in range(1, devices, CORES)
            for p in range(planes)
        ]
        return lax.ppermute(x, ("tok", "mem"), pairs)

    hidden = fast_weights.shape[1]
    rows = hidden // chips
    local_w = lax.dynamic_slice_in_dim(fast_weights, source, memories, 0).astype(BF16)
    sent_w = to_plane(local_w)
    keys, values, local_w = lax.optimization_barrier((keys, values, local_w))
    far_k, far_v = to_far(keys), to_far(values)
    mate_k, mate_v = to_core(keys), to_core(values)
    rates = lax.dynamic_slice_in_dim(step_sizes, plane * memories, memories, 0)
    rates = jnp.pad(rates, ((0, -memories % 8), (0, 0)))
    mate_rates = to_core(rates)
    lengths = view_lengths.reshape(-1, 1)

    near = attend_near(spots, lengths, queries, keys, values, mate_k, mate_v)
    near, sent_w = lax.optimization_barrier((near, sent_w))
    grads = half_grads(
        spots, chips, keys, values, mate_k, mate_v, rates, mate_rates, local_w, sent_w
    )
    local_rows = lax.dynamic_slice(
        fast_weights, (source, chip * rows, 0), (memories, rows, 3 * DM)
    )
    held, local_rows = lax.optimization_barrier((grads, local_rows))
    sent_rows = to_plane(local_rows)
    stride = chips
    for radix in digits[::-1]:
        stride //= radix
        if stride == 1:
            held, far_k, far_v = lax.optimization_barrier((held, far_k, far_v))
        held = held.reshape((radix, stride) + held.shape[1:])
        came = [to_chip(held[step], step * stride) for step in range(1, radix)]
        if stride > 1:
            held = sum([part.astype(F32) for part in came], held[0].astype(F32)).astype(BF16)
    parts = [part[0] for part in [held[0]] + came]
    all_tokens = tokens * devices
    fresh = update_rows(spots, 1.0 / math.sqrt(all_tokens), parts, local_rows, sent_rows)

    gathered = fresh[None]
    for place, radix in enumerate(digits):
        came = [to_chip(gathered, step * stride) for step in range(1, radix)]
        stride *= radix
        if place == len(digits) - 1:
            near, gathered = lax.optimization_barrier((near, gathered))
            attended = attend_far(spots, lengths, queries, far_k, far_v, near)
            came, attended = lax.optimization_barrier((came, attended))
        gathered = jnp.concatenate([gathered] + came, axis=0)
    mate_w = to_core(gathered)

    return read_out(queries, gathered, mate_w, attended)


def solution(mesh):
    placed = (
        P("tok", "mem"),
        P("tok", "mem"),
        P("tok", "mem"),
        P(None, "tok"),
        P(None, "mem", None),
        P(),
    )
    return jax.shard_map(
        on_device, mesh=mesh, in_specs=placed, out_specs=P("tok", "mem"), check_vma=False
    )
```

```python
import functools
import math

import jax
import jax.numpy as jnp
from jax import lax
from jax.experimental import pallas as pl
from jax.experimental.pallas import tpu as pltpu
from jax.sharding import PartitionSpec as P

DM = 256
HD = 128
CORES = 2
NORM_EPS = 1e-06
VMEM_BYTES = 40 * 2**20
MASKED = -1e30

BF16 = jnp.bfloat16
F32 = jnp.float32


def in_vmem(count):
    return [pl.BlockSpec(memory_space=pltpu.VMEM)] * count


def in_smem():
    return pl.BlockSpec(memory_space=pltpu.SMEM)


def params(limit=VMEM_BYTES):
    return pltpu.CompilerParams(vmem_limit_bytes=limit)


def dot_nt(a, b):
    return lax.dot_general(a, b, (((1,), (1,)), ((), ())), preferred_element_type=F32)


def dot_tn(a, b):
    return lax.dot_general(a, b, (((0,), (0,)), ((), ())), preferred_element_type=F32)


def dot_nn(a, b):
    return jnp.dot(a, b, preferred_element_type=F32)


def chip_digits(chips):
    digits = []
    while chips % 4 == 0:
        digits.append(4)
        chips //= 4
    if chips > 1:
        digits.append(chips)
    return digits[::-1]


def from_hbm(*arrays):
    return [pltpu.with_memory_space_constraint(array, pltpu.HBM) for array in arrays]


def stage_kernel(
    blocks, q_any, k_any, v_any, rates_any, weights_any,
    spots, q_ref, pack_ref, far_ref, last_ref, w_ref, give_ref, exact_ref,
    held, rates, sems,
):
    spot, plane = lax.axis_index("tok"), lax.axis_index("mem")
    devices, planes = lax.axis_size("tok"), lax.axis_size("mem")
    tokens, width = q_ref.shape
    memories, hidden, _ = exact_ref.shape
    core, chip = lax.rem(spot, CORES), lax.div(spot, CORES)
    copies = []

    def bring(source, goal):
        copies.append(pltpu.make_async_copy(source, goal, sems.at[len(copies)]))
        copies[-1].start()

    units = pl.ds(pl.multiple_of(core * hidden, hidden), hidden)
    other = planes - 1 - plane
    bring(weights_any.at[pl.ds(other * memories, memories), units], held)
    bring(weights_any.at[pl.ds(plane * memories, memories), units], exact_ref)
    bring(rates_any, rates)
    bring(v_any, pack_ref.at[pl.ds(tokens, tokens)])
    bring(k_any, pack_ref.at[pl.ds(0, tokens)])
    pieces = [part for m in range(memories) for part in ((k_any, m), (v_any, m))]
    for place, (part, m) in enumerate(pieces):
        goal = far_ref.at[pl.ds(place * tokens, tokens)] if place < len(pieces) - 1 else last_ref
        bring(part.at[:, pl.ds(m * DM, DM)], goal)
    bring(q_any, q_ref)
    spots[0] = spot * tokens
    spots[1] = (spot ^ 1) * tokens
    spots[2] = jnp.where(core == 0, spot - 1, spot + 1) * tokens
    spots[3] = lax.div(chip, devices // CORES // blocks)
    copies[0].wait()
    for memory in range(memories):
        give_ref[memory] = held[memory].astype(BF16)
    copies[1].wait()
    for memory in range(memories):
        w_ref[memory] = exact_ref[memory].astype(BF16)
    copies[2].wait()
    copies[3].wait()
    turned = jnp.transpose(rates[...])
    for memory in range(memories):
        rate = jnp.zeros((tokens, 1), F32)
        for here in range(planes):
            place = here * memories + memory
            rate = jnp.where(plane == here, turned[:, place : place + 1], rate)
        features = pl.ds(memory * DM, DM)
        value = pack_ref[pl.ds(tokens, tokens), features]
        pack_ref[pl.ds(2 * tokens, tokens), features] = (rate * value.astype(F32)).astype(BF16)
    for copy in copies[4:]:
        copy.wait()


def stage(queries, keys, values, step_sizes, fast_weights, memories, blocks):
    tokens, width = queries.shape
    half = (memories, fast_weights.shape[1] // CORES, 3 * DM)
    return pl.pallas_call(
        functools.partial(stage_kernel, blocks),
        out_shape=(
            jax.ShapeDtypeStruct((8,), jnp.int32),
            pltpu.VMEM((tokens, width), BF16),
            pltpu.VMEM((3 * tokens, width), BF16),
            pltpu.VMEM(((2 * memories - 1) * tokens, DM), BF16),
            pltpu.VMEM((tokens, DM), BF16),
            pltpu.VMEM(half, BF16),
            pltpu.VMEM(half, BF16),
            pltpu.VMEM(half, F32),
        ),
        in_specs=[pl.BlockSpec(memory_space=pltpu.HBM)] * 5,
        out_specs=(in_smem(),) + tuple(in_vmem(7)),
        scratch_shapes=[
            pltpu.VMEM(half, F32),
            pltpu.VMEM(step_sizes.shape, F32),
            pltpu.SemaphoreType.DMA((6 + 2 * memories,)),
        ],
        compiler_params=params(),
    )(*from_hbm(queries, keys, values, step_sizes, fast_weights))


def grads_kernel(spots, own, mate, own_w, sent_w, grad_ref):
    tokens = own.shape[0] // 3
    memories = own_w.shape[0]
    hidden = 2 * own_w.shape[1]
    for memory in range(memories):
        features = pl.ds(memory * DM, DM)
        weights = jnp.concatenate([own_w[memory], sent_w[memory]], axis=0)
        gate_up_w = jnp.concatenate([weights[:, :DM], weights[:, DM : 2 * DM]], axis=0)
        out_w = weights[:, 2 * DM :]
        grad_pair = jnp.zeros((2 * hidden, DM), F32)
        grad_out = jnp.zeros((hidden, DM), F32)
        for side in (own, mate):
            key = side[pl.ds(0, tokens), features]
            scaled = side[pl.ds(2 * tokens, tokens), features]
            gate_up = dot_nt(key, gate_up_w)
            gate, up = gate_up[:, :hidden], gate_up[:, hidden:]
            sigmoid = jax.nn.sigmoid(gate)
            swish = gate * sigmoid
            slope = sigmoid * (1.0 + gate * (1.0 - sigmoid))
            back = -dot_nt(scaled, out_w)
            pair = jnp.concatenate(
                [(back * up * slope).astype(BF16), (back * swish).astype(BF16)], axis=1
            )
            grad_pair += dot_tn(pair, key)
            grad_out -= dot_tn((swish * up).astype(BF16), scaled)
        found = (grad_pair[:hidden], grad_pair[hidden:], grad_out)
        for part, grad in enumerate(found):
            grad = grad.astype(BF16)
            columns = pl.ds(part * DM, DM)
            if grad_ref.ndim == 3:
                grad_ref[memory, :, columns] = grad
            else:
                blocks, _, rows, _ = grad_ref.shape
                for block in range(blocks):
                    piece = grad[block * rows : (block + 1) * rows]
                    grad_ref[spots[3] ^ block, memory, :, columns] = piece


def half_grads(spots, blocks, own, mate, own_w, sent_w):
    memories, quarter, width = own_w.shape
    hidden = 2 * quarter
    rows = hidden // blocks
    placed = rows % 16 == 0
    shape = (blocks, memories, rows, width) if placed else (memories, hidden, width)
    grads = pl.pallas_call(
        grads_kernel,
        out_shape=jax.ShapeDtypeStruct(shape, BF16),
        in_specs=[in_smem()] + in_vmem(4),
        out_specs=in_vmem(1)[0],
        compiler_params=params(),
    )(spots, own, mate, own_w, sent_w)
    if placed:
        return grads
    grads = grads.reshape(memories, blocks, rows, width).transpose(1, 0, 2, 3)
    return jnp.take(grads, jnp.arange(blocks, dtype=jnp.int32) ^ spots[3], axis=0)


def update_kernel(step_rate, parts, spots, *refs):
    *grads, exact, sent, new_ref = refs
    rows = new_ref.shape[1]
    total = grads[0][...].astype(F32)
    for part in grads[1:]:
        total += part[...].astype(F32)
    if sent is None:
        before = exact[...]
    else:
        held = exact.shape[1]
        first = spots[3] * rows
        near = pl.multiple_of(jnp.minimum(first, held - rows), rows)
        away = pl.multiple_of(jnp.maximum(first - held, 0), rows)
        before = jnp.where(
            first < held, exact[:, pl.ds(near, rows), :], sent[:, pl.ds(away, rows), :].astype(F32)
        )
    stepped = before - total * step_rate
    for block in range(3):
        columns = slice(block * DM, (block + 1) * DM)
        old, new = before[..., columns], stepped[..., columns]
        old_norm = jnp.sqrt(jnp.sum(old * old, axis=-1, keepdims=True))
        new_norm = jnp.sqrt(jnp.sum(new * new, axis=-1, keepdims=True) + NORM_EPS)
        new_ref[:, :, columns] = (new * (old_norm / new_norm)).astype(BF16)


def update_rows(spots, step_rate, grads, exact, sent):
    rows = grads[0].shape[1]
    body = functools.partial(update_kernel, step_rate, len(grads))
    given = list(grads) + [exact, sent]
    if rows % 16:
        whole = jnp.concatenate([exact, sent.astype(F32)], axis=1)
        given[-2:] = [lax.dynamic_slice_in_dim(whole, spots[3] * rows, rows, 1)]

        def body(spots, *refs):
            update_kernel(step_rate, len(grads), spots, *refs[:-1], None, refs[-1])

    return pl.pallas_call(
        body,
        out_shape=jax.ShapeDtypeStruct(grads[0].shape, BF16),
        in_specs=[in_smem()] + in_vmem(len(given)),
        out_specs=in_vmem(1)[0],
        compiler_params=params(),
    )(spots, *given)


def view_bounds(lengths, own, tokens):
    views = lengths.shape[1]
    down = lax.broadcasted_iota(jnp.int32, (views, views), 0)
    across = lax.broadcasted_iota(jnp.int32, (views, views), 1)
    column = jnp.sum(jnp.where(down == across, lengths[...], 0), axis=1, keepdims=True)
    ends = jnp.sum(jnp.where(down <= across, column, 0), axis=0, keepdims=True)
    spot = own + lax.broadcasted_iota(jnp.int32, (tokens, 1), 0)
    stop = jnp.min(jnp.where(ends > spot, ends, jnp.int32(2**30)), axis=1, keepdims=True)
    start = jnp.max(jnp.where(ends <= spot, ends, 0), axis=1, keepdims=True)
    return start, stop


def inside(base, count, start, stop):
    place = base + lax.broadcasted_iota(jnp.int32, (1, count), 1)
    return (place >= start) & (place < stop)


SCORE_SCALE = math.log2(math.e) / math.sqrt(HD)


def near_kernel(spots, lengths, q_ref, own, mate, mixed_ref, peak_ref, sum_ref):
    tokens, width = q_ref.shape
    start, stop = view_bounds(lengths, spots[0], tokens)
    block_rows = tokens // 2
    for block in range(2):
        rows = slice(block * block_rows, (block + 1) * block_rows)
        masks = [inside(spots[i], tokens, start[rows], stop[rows]) for i in range(2)]
        for head in range(width // HD):
            lanes = pl.ds(head * HD, HD)
            query = q_ref[rows, lanes]
            scores = [
                jnp.where(mask, dot_nt(query, side[:tokens, lanes]) * SCORE_SCALE, MASKED)
                for mask, side in zip(masks, (own, mate))
            ]
            peak = functools.reduce(
                jnp.maximum, [jnp.max(s, axis=1, keepdims=True) for s in scores]
            )
            weights = [jnp.exp2(s - peak) for s in scores]
            peak_ref[rows, head : head + 1] = peak
            sum_ref[rows, head : head + 1] = sum(
                jnp.sum(w, axis=1, keepdims=True) for w in weights
            )
            mixed_ref[rows, lanes] = sum(
                dot_nn(w.astype(BF16), side[pl.ds(tokens, tokens), lanes])
                for w, side in zip(weights, (own, mate))
            )


def far_kernel(
    memory, spots, lengths, q_ref, far, last, mixed_ref, peak_ref, sum_ref, out_ref
):
    tokens, _ = q_ref.shape
    start, stop = view_bounds(lengths, spots[0], tokens)
    far_k = far.at[pl.ds(2 * memory * tokens, tokens)]
    far_v = last if last is not None else far.at[pl.ds((2 * memory + 1) * tokens, tokens)]
    block_rows = tokens // 2
    for block in range(2):
        rows = slice(block * block_rows, (block + 1) * block_rows)
        mask = inside(spots[2], tokens, start[rows], stop[rows])
        for step in range(DM // HD):
            lanes = pl.ds(step * HD, HD)
            head = memory * (DM // HD) + step
            across = pl.ds(head * HD, HD)
            scores = dot_nt(q_ref[rows, across], far_k[:, lanes]) * SCORE_SCALE
            scores = jnp.where(mask, scores, MASKED)
            before = peak_ref[rows, head : head + 1]
            peak = jnp.maximum(before, jnp.max(scores, axis=1, keepdims=True))
            weights = jnp.exp2(scores - peak)
            shrink = jnp.exp2(before - peak)
            total = sum_ref[rows, head : head + 1] * shrink + jnp.sum(
                weights, axis=1, keepdims=True
            )
            mixed = mixed_ref[rows, across] * shrink + dot_nn(
                weights.astype(BF16), far_v[:, lanes]
            )
            out_ref[rows, lanes] = mixed / total


def attend_near(spots, lengths, queries, own, mate):
    tokens, width = queries.shape
    stats = jax.ShapeDtypeStruct((tokens, width // HD), F32)
    return pl.pallas_call(
        near_kernel,
        out_shape=(jax.ShapeDtypeStruct(queries.shape, F32), stats, stats),
        in_specs=[in_smem()] + in_vmem(4),
        out_specs=tuple(in_vmem(3)),
        compiler_params=params(),
    )(spots, lengths, queries, own, mate)


def attend_far(memory, spots, lengths, queries, far, last, near):
    if last is None:

        def body(spots, lengths, q_ref, far, *rest):
            far_kernel(memory, spots, lengths, q_ref, far, None, *rest)
    else:
        body = functools.partial(far_kernel, memory)
    given = (lengths, queries, far) + (() if last is None else (last,)) + tuple(near)
    return pl.pallas_call(
        body,
        out_shape=jax.ShapeDtypeStruct((queries.shape[0], DM), F32),
        in_specs=[in_smem()] + in_vmem(len(given)),
        out_specs=in_vmem(1)[0],
        compiler_params=params(),
    )(spots, *given)


def read_kernel(parts, q_ref, w_ref, *refs):
    before, out_ref = refs[:parts], refs[parts]
    blocks, memories, rows, _ = w_ref.shape
    for memory in range(memories):
        features = pl.ds(memory * DM, DM)
        query = q_ref[:, features]
        weights = w_ref[:, memory].reshape(blocks * rows, 3 * DM)
        gate = dot_nt(query, weights[:, :DM])
        up = dot_nt(query, weights[:, DM : 2 * DM])
        hidden = (gate * jax.nn.sigmoid(gate) * up).astype(BF16)
        total = dot_nn(hidden, weights[:, 2 * DM :])
        if parts > 0:
            total += before[0][:, features] + before[1 + memory][...]
        out_ref[:, features] = total.astype(out_ref.dtype)


def read_half(queries, weights, before, kind):
    return pl.pallas_call(
        functools.partial(read_kernel, len(before)),
        out_shape=jax.ShapeDtypeStruct(queries.shape, kind),
        in_specs=in_vmem(2 + len(before)),
        out_specs=in_vmem(1)[0],
        compiler_params=params(),
    )(queries, weights, *before)


def on_device(queries, keys, values, step_sizes, fast_weights, view_lengths):
    tokens = queries.shape[0]
    memories = queries.shape[1] // DM
    devices = lax.axis_size("tok")
    planes = lax.axis_size("mem")
    chips = devices // CORES
    digits = chip_digits(chips)
    blocks = chips // digits[0]

    def to_core(x):
        return lax.ppermute(x, "tok", [(i, i ^ 1) for i in range(devices)])

    def to_far(x):
        return lax.ppermute(x, "tok", [(i, (i + i % 2 * 2 - 1) % devices) for i in range(devices)])

    def to_chip(x, flip):
        pairs = [(i, (((i // CORES) ^ flip) * CORES) + i % CORES) for i in range(devices)]
        return lax.ppermute(x, "tok", pairs)

    def to_plane(x):
        return lax.ppermute(x, "mem", [(p, planes - 1 - p) for p in range(planes)])

    spots, q, own, far, last, own_w, give_w, exact = stage(
        queries, keys, values, step_sizes, fast_weights, memories, blocks
    )
    sent_w = to_plane(give_w)
    mate = to_core(own)
    far = to_far(far)
    lengths = view_lengths.reshape(1, -1)

    held = half_grads(spots, blocks, own, mate, own_w, sent_w)
    held, q = lax.optimization_barrier((held, q))
    near = attend_near(spots, lengths, q, own, mate)
    stride = chips
    for place, radix in enumerate(digits[:0:-1]):
        stride //= radix
        held = held.reshape((radix, stride // digits[0]) + held.shape[1:])
        came = [to_chip(held[step], step * stride) for step in range(1, radix)]
        if place == 0:
            came, near, far = lax.optimization_barrier((came, near, far))
        held = sum([part.astype(F32) for part in came], held[0].astype(F32)).astype(BF16)
    held = held[0]
    came = [to_chip(held, step) for step in range(1, digits[0])]
    came, last = lax.optimization_barrier((came, last))
    last = to_far(last)
    all_tokens = tokens * devices
    fresh = update_rows(
        spots, 1.0 / math.sqrt(all_tokens), [held] + came, exact, sent_w
    )

    gathered = fresh[None]
    stride = digits[0]
    for radix in digits[1:]:
        came = [to_chip(gathered, step * stride) for step in range(1, radix)]
        if stride == digits[0]:
            gathered, near = lax.optimization_barrier((gathered, near))
            attended = [
                attend_far(m, spots, lengths, q, far, last if m == memories - 1 else None, near)
                for m in range(memories)
            ]
            came, attended = lax.optimization_barrier((came, attended))
        stride *= radix
        gathered = jnp.concatenate([gathered] + came, axis=0)
    mate_w = to_core(gathered)
    partial = read_half(q, gathered, [], F32)
    return read_half(q, mate_w, [partial] + attended, BF16)


def solution(mesh):
    placed = (
        P("tok", "mem"),
        P("tok", "mem"),
        P("tok", "mem"),
        P(None, "tok"),
        P(None, "mem", None),
        P(),
    )
    return jax.shard_map(
        on_device, mesh=mesh, in_specs=placed, out_specs=P("tok", "mem"), check_vma=False
    )
```

```python
import functools
import math

import jax
import jax.numpy as jnp
from jax import lax
from jax.experimental import pallas as pl
from jax.experimental.pallas import tpu as pltpu
from jax.sharding import PartitionSpec as P

DM = 256
HD = 128
CORES = 2
NORM_EPS = 1e-06
VMEM_BYTES = 40 * 2**20
MASKED = -1e30

BF16 = jnp.bfloat16
F32 = jnp.float32


def in_vmem(count):
    return [pl.BlockSpec(memory_space=pltpu.VMEM)] * count


def in_smem():
    return pl.BlockSpec(memory_space=pltpu.SMEM)


def params(limit=VMEM_BYTES):
    return pltpu.CompilerParams(vmem_limit_bytes=limit)


def dot_nt(a, b):
    return lax.dot_general(a, b, (((1,), (1,)), ((), ())), preferred_element_type=F32)


def dot_tn(a, b):
    return lax.dot_general(a, b, (((0,), (0,)), ((), ())), preferred_element_type=F32)


def dot_nn(a, b):
    return jnp.dot(a, b, preferred_element_type=F32)


def chip_digits(chips):
    digits = []
    while chips % 4 == 0:
        digits.append(4)
        chips //= 4
    if chips > 1:
        digits.append(chips)
    return digits[::-1]


def from_hbm(*arrays):
    return [pltpu.with_memory_space_constraint(array, pltpu.HBM) for array in arrays]


def stage_kernel(
    blocks, q_any, k_any, v_any, rates_any, weights_any,
    spots, q_ref, pack_ref, far_ref, last_ref, w_ref, give_ref, exact_ref,
    held, rates, sems,
):
    spot, plane = lax.axis_index("tok"), lax.axis_index("mem")
    devices, planes = lax.axis_size("tok"), lax.axis_size("mem")
    tokens, width = q_ref.shape
    memories, hidden, _ = exact_ref.shape
    core, chip = lax.rem(spot, CORES), lax.div(spot, CORES)
    copies = []

    def bring(source, goal):
        copies.append(pltpu.make_async_copy(source, goal, sems.at[len(copies)]))
        copies[-1].start()

    units = pl.ds(pl.multiple_of(core * hidden, hidden), hidden)
    other = planes - 1 - plane
    bring(weights_any.at[pl.ds(other * memories, memories), units], held)
    bring(weights_any.at[pl.ds(plane * memories, memories), units], exact_ref)
    bring(rates_any, rates)
    bring(v_any, pack_ref.at[pl.ds(tokens, tokens)])
    bring(k_any, pack_ref.at[pl.ds(0, tokens)])
    pieces = [part for m in range(memories) for part in ((k_any, m), (v_any, m))]
    for place, (part, m) in enumerate(pieces):
        goal = far_ref.at[pl.ds(place * tokens, tokens)] if place < len(pieces) - 1 else last_ref
        bring(part.at[:, pl.ds(m * DM, DM)], goal)
    bring(q_any, q_ref)
    spots[0] = spot * tokens
    spots[1] = (spot ^ 1) * tokens
    spots[2] = jnp.where(core == 0, spot - 1, spot + 1) * tokens
    spots[3] = lax.div(chip, devices // CORES // blocks)
    copies[0].wait()
    for memory in range(memories):
        give_ref[memory] = held[memory].astype(BF16)
    copies[1].wait()
    for memory in range(memories):
        w_ref[memory] = exact_ref[memory].astype(BF16)
    copies[2].wait()
    copies[3].wait()
    turned = jnp.transpose(rates[...])
    for memory in range(memories):
        rate = jnp.zeros((tokens, 1), F32)
        for here in range(planes):
            place = here * memories + memory
            rate = jnp.where(plane == here, turned[:, place : place + 1], rate)
        features = pl.ds(memory * DM, DM)
        value = pack_ref[pl.ds(tokens, tokens), features]
        pack_ref[pl.ds(2 * tokens, tokens), features] = (rate * value.astype(F32)).astype(BF16)
    for copy in copies[4:]:
        copy.wait()


def stage(queries, keys, values, step_sizes, fast_weights, memories, blocks):
    tokens, width = queries.shape
    half = (memories, fast_weights.shape[1] // CORES, 3 * DM)
    return pl.pallas_call(
        functools.partial(stage_kernel, blocks),
        out_shape=(
            jax.ShapeDtypeStruct((8,), jnp.int32),
            pltpu.VMEM((tokens, width), BF16),
            pltpu.VMEM((3 * tokens, width), BF16),
            pltpu.VMEM(((2 * memories - 1) * tokens, DM), BF16),
            pltpu.VMEM((tokens, DM), BF16),
            pltpu.VMEM(half, BF16),
            pltpu.VMEM(half, BF16),
            pltpu.VMEM(half, F32),
        ),
        in_specs=[pl.BlockSpec(memory_space=pltpu.HBM)] * 5,
        out_specs=(in_smem(),) + tuple(in_vmem(7)),
        scratch_shapes=[
            pltpu.VMEM(half, F32),
            pltpu.VMEM(step_sizes.shape, F32),
            pltpu.SemaphoreType.DMA((6 + 2 * memories,)),
        ],
        compiler_params=params(),
    )(*from_hbm(queries, keys, values, step_sizes, fast_weights))


def grads_kernel(spots, own, mate, own_w, sent_w, grad_ref):
    tokens = own.shape[0] // 3
    memories, quarter, _ = own_w.shape
    hidden = 2 * quarter
    for memory in range(memories):
        features = pl.ds(memory * DM, DM)
        weights = jnp.concatenate([own_w[memory], sent_w[memory]], axis=0)
        gate_up_w = jnp.concatenate([weights[:, :DM], weights[:, DM : 2 * DM]], axis=0)
        out_w = weights[:, 2 * DM :]
        grad_pair = jnp.zeros((2 * hidden, DM), F32)
        grad_out = jnp.zeros((hidden, DM), F32)
        for side in (own, mate):
            key = side[pl.ds(0, tokens), features]
            scaled = side[pl.ds(2 * tokens, tokens), features]
            gate_up = dot_nt(gate_up_w, key)
            gate, up = gate_up[:hidden], gate_up[hidden:]
            sigmoid = jax.nn.sigmoid(gate)
            swish = gate * sigmoid
            slope = sigmoid * (1.0 + gate * (1.0 - sigmoid))
            back = -dot_nt(out_w, scaled)
            pair = jnp.concatenate(
                [(back * up * slope).astype(BF16), (back * swish).astype(BF16)], axis=0
            )
            grad_pair += dot_nn(pair, key)
            grad_out -= dot_nn((swish * up).astype(BF16), scaled)
        found = (grad_pair[:hidden], grad_pair[hidden:], grad_out)
        for part, grad in enumerate(found):
            grad = grad.astype(BF16)
            columns = pl.ds(part * DM, DM)
            if grad_ref.ndim == 3:
                grad_ref[memory, :, columns] = grad
            else:
                blocks, _, rows, _ = grad_ref.shape
                rows //= 2
                for block in range(blocks):
                    for half in range(2):
                        first = half * quarter + block * rows
                        piece = grad[first : first + rows]
                        owned = pl.ds(half * rows, rows)
                        grad_ref[spots[3] ^ block, memory, owned, columns] = piece


def half_grads(spots, blocks, own, mate, own_w, sent_w):
    memories, quarter, width = own_w.shape
    rows = quarter // blocks
    placed = rows % 16 == 0
    shape = (blocks, memories, 2 * rows, width) if placed else (memories, 2 * quarter, width)
    grads = pl.pallas_call(
        grads_kernel,
        out_shape=jax.ShapeDtypeStruct(shape, BF16),
        in_specs=[in_smem()] + in_vmem(4),
        out_specs=in_vmem(1)[0],
        compiler_params=params(),
    )(spots, own, mate, own_w, sent_w)
    if placed:
        return grads
    grads = grads.reshape(memories, 2, blocks, rows, width).transpose(2, 0, 1, 3, 4)
    grads = grads.reshape(blocks, memories, 2 * rows, width)
    return jnp.take(grads, jnp.arange(blocks, dtype=jnp.int32) ^ spots[3], axis=0)


def update_kernel(step_rate, parts, spots, *refs):
    *grads, exact, sent, new_ref = refs
    rows = new_ref.shape[1] // 2
    if exact.shape[1] == rows:
        here = pl.ds(0, rows)
    else:
        here = pl.ds(pl.multiple_of(spots[3] * rows, rows), rows)
    for half, held in enumerate((exact, sent)):
        owned = pl.ds(half * rows, rows)
        total = grads[0][:, owned, :].astype(F32)
        for part in grads[1:]:
            total += part[:, owned, :].astype(F32)
        before = held[:, here, :].astype(F32)
        stepped = before - total * step_rate
        for block in range(3):
            columns = slice(block * DM, (block + 1) * DM)
            old, new = before[..., columns], stepped[..., columns]
            old_norm = jnp.sqrt(jnp.sum(old * old, axis=-1, keepdims=True))
            new_norm = jnp.sqrt(jnp.sum(new * new, axis=-1, keepdims=True) + NORM_EPS)
            new_ref[:, owned, columns] = (new * (old_norm / new_norm)).astype(BF16)


def update_rows(spots, step_rate, grads, exact, sent):
    rows = grads[0].shape[1] // 2
    if rows % 16:
        exact, sent = (
            lax.dynamic_slice_in_dim(held, spots[3] * rows, rows, 1) for held in (exact, sent)
        )
    given = list(grads) + [exact, sent]
    return pl.pallas_call(
        functools.partial(update_kernel, step_rate, len(grads)),
        out_shape=jax.ShapeDtypeStruct(grads[0].shape, BF16),
        in_specs=[in_smem()] + in_vmem(len(given)),
        out_specs=in_vmem(1)[0],
        compiler_params=params(),
    )(spots, *given)


def view_bounds(lengths, own, tokens):
    views = lengths.shape[1]
    down = lax.broadcasted_iota(jnp.int32, (views, views), 0)
    across = lax.broadcasted_iota(jnp.int32, (views, views), 1)
    column = jnp.sum(jnp.where(down == across, lengths[...], 0), axis=1, keepdims=True)
    ends = jnp.sum(jnp.where(down <= across, column, 0), axis=0, keepdims=True)
    spot = own + lax.broadcasted_iota(jnp.int32, (tokens, 1), 0)
    stop = jnp.min(jnp.where(ends > spot, ends, jnp.int32(2**30)), axis=1, keepdims=True)
    start = jnp.max(jnp.where(ends <= spot, ends, 0), axis=1, keepdims=True)
    return start, stop


def inside(base, start, stop):
    place = base + lax.broadcasted_iota(jnp.int32, start.shape, 1)
    return jnp.where((place >= start) & (place < stop), 0.0, MASKED)


SCORE_SCALE = math.log2(math.e) / math.sqrt(HD)


def lanes_wide(column, count):
    return jnp.concatenate([column] * (count // HD), axis=1) if count > HD else column


def summing(values):
    return jnp.concatenate([values, jnp.ones_like(values)], axis=1)


def near_kernel(spots, lengths, q_ref, own, mate, mixed_ref, peak_ref, sum_ref, bound_ref):
    tokens, width = q_ref.shape
    bounds = [
        jnp.broadcast_to(bound, (tokens, HD)) for bound in view_bounds(lengths, spots[0], tokens)
    ]
    bound_ref[0], bound_ref[1] = bounds
    block_rows = tokens // 4
    for block in range(4):
        rows = slice(block * block_rows, (block + 1) * block_rows)
        start, stop = (lanes_wide(bound[rows], tokens) for bound in bounds)
        shifts = [inside(spots[i], start, stop) for i in range(2)]
        for head in range(width // HD):
            lanes = pl.ds(head * HD, HD)
            query = q_ref[rows, lanes]
            scores = [
                dot_nt(query, side[:tokens, lanes]) + shift
                for shift, side in zip(shifts, (own, mate))
            ]
            peak = jnp.max(jnp.maximum(*scores), axis=1, keepdims=True)
            mixed = sum(
                dot_nn(
                    jnp.exp2((score - peak) * SCORE_SCALE).astype(BF16),
                    summing(side[pl.ds(tokens, tokens), lanes]),
                )
                for score, side in zip(scores, (own, mate))
            )
            mixed_ref[rows, lanes] = mixed[:, :HD]
            peak_ref[head, rows] = jnp.broadcast_to(peak, (block_rows, HD))
            sum_ref[head, rows] = mixed[:, HD:]


def far_kernel(memory, spots, q_ref, far, last, mixed_ref, peak_ref, sum_ref, bound_ref, out_ref):
    tokens, _ = q_ref.shape
    far_k = far.at[pl.ds(2 * memory * tokens, tokens)]
    far_v = last if last is not None else far.at[pl.ds((2 * memory + 1) * tokens, tokens)]
    block_rows = tokens // 4
    for block in range(4):
        rows = slice(block * block_rows, (block + 1) * block_rows)
        start, stop = (lanes_wide(bound_ref[i, rows], tokens) for i in range(2))
        shift = inside(spots[2], start, stop)
        for step in range(DM // HD):
            lanes = pl.ds(step * HD, HD)
            head = memory * (DM // HD) + step
            across = pl.ds(head * HD, HD)
            scores = dot_nt(q_ref[rows, across], far_k[:, lanes]) + shift
            before = peak_ref[head, rows]
            peak = jnp.maximum(before, jnp.max(scores, axis=1, keepdims=True))
            weights = jnp.exp2((scores - lanes_wide(peak, tokens)) * SCORE_SCALE)
            shrink = jnp.exp2((before - peak) * SCORE_SCALE)
            mixed = dot_nn(weights.astype(BF16), summing(far_v[:, lanes]))
            total = sum_ref[head, rows] * shrink + mixed[:, HD:]
            out_ref[rows, lanes] = (mixed_ref[rows, across] * shrink + mixed[:, :HD]) / total


def attend_near(spots, lengths, queries, own, mate):
    tokens, width = queries.shape
    stats = jax.ShapeDtypeStruct((width // HD, tokens, HD), F32)
    bounds = jax.ShapeDtypeStruct((2, tokens, HD), jnp.int32)
    return pl.pallas_call(
        near_kernel,
        out_shape=(jax.ShapeDtypeStruct(queries.shape, F32), stats, stats, bounds),
        in_specs=[in_smem()] + in_vmem(4),
        out_specs=tuple(in_vmem(4)),
        compiler_params=params(),
    )(spots, lengths, queries, own, mate)


def attend_far(memory, spots, queries, far, last, near):
    if last is None:

        def body(spots, q_ref, far, *rest):
            far_kernel(memory, spots, q_ref, far, None, *rest)
    else:
        body = functools.partial(far_kernel, memory)
    given = (queries, far) + (() if last is None else (last,)) + tuple(near)
    return pl.pallas_call(
        body,
        out_shape=jax.ShapeDtypeStruct((queries.shape[0], DM), F32),
        in_specs=[in_smem()] + in_vmem(len(given)),
        out_specs=in_vmem(1)[0],
        compiler_params=params(),
    )(spots, *given)


def read_kernel(parts, q_ref, w_ref, *refs):
    before, out_ref = refs[:parts], refs[parts]
    blocks, memories, rows, _ = w_ref.shape
    for memory in range(memories):
        features = pl.ds(memory * DM, DM)
        query = q_ref[:, features]
        weights = w_ref[:, memory].reshape(blocks * rows, 3 * DM)
        gate = dot_nt(query, weights[:, :DM])
        up = dot_nt(query, weights[:, DM : 2 * DM])
        hidden = (gate * jax.nn.sigmoid(gate) * up).astype(BF16)
        total = dot_nn(hidden, weights[:, 2 * DM :])
        if parts > 0:
            total += before[0][:, features] + before[1 + memory][...]
        out_ref[:, features] = total.astype(out_ref.dtype)


def read_half(queries, weights, before, kind):
    return pl.pallas_call(
        functools.partial(read_kernel, len(before)),
        out_shape=jax.ShapeDtypeStruct(queries.shape, kind),
        in_specs=in_vmem(2 + len(before)),
        out_specs=in_vmem(1)[0],
        compiler_params=params(),
    )(queries, weights, *before)


def on_device(queries, keys, values, step_sizes, fast_weights, view_lengths):
    tokens = queries.shape[0]
    memories = queries.shape[1] // DM
    devices = lax.axis_size("tok")
    planes = lax.axis_size("mem")
    chips = devices // CORES
    digits = chip_digits(chips)
    blocks = chips // digits[0]

    def to_core(x):
        return lax.ppermute(x, "tok", [(i, i ^ 1) for i in range(devices)])

    def to_far(x):
        pairs = [
            (i * planes + p, (i + i % 2 * 2 - 1) * planes + p)
            for i in range(1, devices - 1)
            for p in range(planes)
        ]
        for i in (0, devices - 1):
            pairs += [(i * planes + p, i * planes + planes - 1 - p) for p in range(planes)]
        return lax.ppermute(x, ("tok", "mem"), pairs)

    def to_chip(x, flip):
        pairs = [(i, (((i // CORES) ^ flip) * CORES) + i % CORES) for i in range(devices)]
        return lax.ppermute(x, "tok", pairs)

    def to_plane(x):
        return lax.ppermute(x, "mem", [(p, planes - 1 - p) for p in range(planes)])

    spots, q, own, far, last, own_w, give_w, exact = stage(
        queries, keys, values, step_sizes, fast_weights, memories, blocks
    )
    sent_w = to_plane(give_w)
    mate = to_core(own)
    far = to_far(far)
    lengths = view_lengths.reshape(1, -1)

    held = half_grads(spots, blocks, own, mate, own_w, sent_w)
    held, q = lax.optimization_barrier((held, q))
    near = attend_near(spots, lengths, q, own, mate)
    stride = chips
    for place, radix in enumerate(digits[:0:-1]):
        stride //= radix
        held = held.reshape((radix, stride // digits[0]) + held.shape[1:])
        came = [to_chip(held[step], step * stride) for step in range(1, radix)]
        if place == 0:
            came, near = lax.optimization_barrier((came, near))
        held = sum([part.astype(F32) for part in came], held[0].astype(F32)).astype(BF16)
    held = held[0]
    came = [to_chip(held, step) for step in range(1, digits[0])]
    came, last, far = lax.optimization_barrier((came, last, far))
    last = to_far(last)
    all_tokens = tokens * devices
    fresh = update_rows(
        spots, 1.0 / math.sqrt(all_tokens), [held] + came, exact, sent_w
    )

    gathered = fresh[None]
    stride = digits[0]
    for radix in digits[1:]:
        came = [to_chip(gathered, step * stride) for step in range(1, radix)]
        if stride == digits[0]:
            gathered, near = lax.optimization_barrier((gathered, near))
            attended = [
                attend_far(m, spots, q, far, last if m == memories - 1 else None, near)
                for m in range(memories)
            ]
            came, attended = lax.optimization_barrier((came, attended))
        stride *= radix
        gathered = jnp.concatenate([gathered] + came, axis=0)
    mate_w = to_core(gathered)
    partial = read_half(q, gathered, [], F32)
    return read_half(q, mate_w, [partial] + attended, BF16)


def solution(mesh):
    placed = (
        P("tok", "mem"),
        P("tok", "mem"),
        P("tok", "mem"),
        P(None, "tok"),
        P(None, "mem", None),
        P(),
    )
    return jax.shard_map(
        on_device, mesh=mesh, in_specs=placed, out_specs=P("tok", "mem"), check_vma=False
    )
```

```python
import functools
import math

import jax
import jax.numpy as jnp
from jax import lax
from jax.experimental import pallas as pl
from jax.experimental.pallas import tpu as pltpu
from jax.sharding import PartitionSpec as P

DM = 256
HD = 128
CORES = 2
NORM_EPS = 1e-06
VMEM_BYTES = 40 * 2**20
MASKED = -1e30

BF16 = jnp.bfloat16
F32 = jnp.float32


def in_vmem(count):
    return [pl.BlockSpec(memory_space=pltpu.VMEM)] * count


def in_smem():
    return pl.BlockSpec(memory_space=pltpu.SMEM)


def params(limit=VMEM_BYTES):
    return pltpu.CompilerParams(vmem_limit_bytes=limit)


def dot_nt(a, b):
    return lax.dot_general(a, b, (((1,), (1,)), ((), ())), preferred_element_type=F32)


def dot_tn(a, b):
    return lax.dot_general(a, b, (((0,), (0,)), ((), ())), preferred_element_type=F32)


def dot_nn(a, b):
    return jnp.dot(a, b, preferred_element_type=F32)


def chip_digits(chips):
    digits = []
    while chips % 4 == 0:
        digits.append(4)
        chips //= 4
    if chips > 1:
        digits.append(chips)
    return digits[::-1]


def from_hbm(*arrays):
    return [pltpu.with_memory_space_constraint(array, pltpu.HBM) for array in arrays]


def stage_kernel(
    blocks, k_any, v_any, rates_any, weights_any,
    spots, pack_ref, far_ref, w_ref, give_ref, exact_ref,
    held, rates, sems,
):
    spot, plane = lax.axis_index("tok"), lax.axis_index("mem")
    devices, planes = lax.axis_size("tok"), lax.axis_size("mem")
    tokens = pack_ref.shape[0] // 3
    memories, hidden, _ = exact_ref.shape
    core, chip = lax.rem(spot, CORES), lax.div(spot, CORES)
    copies = []

    def bring(source, goal):
        copies.append(pltpu.make_async_copy(source, goal, sems.at[len(copies)]))
        copies[-1].start()

    units = pl.ds(pl.multiple_of(core * hidden, hidden), hidden)
    other = planes - 1 - plane
    bring(weights_any.at[pl.ds(other * memories, memories), units], held)
    bring(weights_any.at[pl.ds(plane * memories, memories), units], exact_ref)
    bring(rates_any, rates)
    bring(v_any, pack_ref.at[pl.ds(tokens, tokens)])
    bring(k_any, pack_ref.at[pl.ds(0, tokens)])
    pieces = [part for m in range(memories) for part in ((k_any, m), (v_any, m))]
    for place, (part, m) in enumerate(pieces[:-1]):
        bring(part.at[:, pl.ds(m * DM, DM)], far_ref.at[pl.ds(place * tokens, tokens)])
    spots[0] = spot * tokens
    spots[1] = (spot ^ 1) * tokens
    spots[2] = jnp.where(core == 0, spot - 1, spot + 1) * tokens
    spots[3] = lax.div(chip, devices // CORES // blocks)
    copies[0].wait()
    for memory in range(memories):
        give_ref[memory] = held[memory].astype(BF16)
    copies[1].wait()
    for memory in range(memories):
        w_ref[memory] = exact_ref[memory].astype(BF16)
    copies[2].wait()
    copies[3].wait()
    turned = jnp.transpose(rates[...])
    for memory in range(memories):
        rate = jnp.zeros((tokens, 1), F32)
        for here in range(planes):
            place = here * memories + memory
            rate = jnp.where(plane == here, turned[:, place : place + 1], rate)
        features = pl.ds(memory * DM, DM)
        value = pack_ref[pl.ds(tokens, tokens), features]
        pack_ref[pl.ds(2 * tokens, tokens), features] = (rate * value.astype(F32)).astype(BF16)
    for copy in copies[4:]:
        copy.wait()


def stage(keys, values, step_sizes, fast_weights, memories, blocks):
    tokens, width = keys.shape
    half = (memories, fast_weights.shape[1] // CORES, 3 * DM)
    return pl.pallas_call(
        functools.partial(stage_kernel, blocks),
        out_shape=(
            jax.ShapeDtypeStruct((8,), jnp.int32),
            pltpu.VMEM((3 * tokens, width), BF16),
            pltpu.VMEM(((2 * memories - 1) * tokens, DM), BF16),
            pltpu.VMEM(half, BF16),
            pltpu.VMEM(half, BF16),
            pltpu.VMEM(half, F32),
        ),
        in_specs=[pl.BlockSpec(memory_space=pltpu.HBM)] * 4,
        out_specs=(in_smem(),) + tuple(in_vmem(5)),
        scratch_shapes=[
            pltpu.VMEM(half, F32),
            pltpu.VMEM(step_sizes.shape, F32),
            pltpu.SemaphoreType.DMA((4 + 2 * memories,)),
        ],
        compiler_params=params(),
    )(*from_hbm(keys, values, step_sizes, fast_weights))


def grads_kernel(spots, own, mate, own_w, sent_w, grad_ref):
    tokens = own.shape[0] // 3
    memories, quarter, _ = own_w.shape
    hidden = 2 * quarter
    for memory in range(memories):
        features = pl.ds(memory * DM, DM)
        weights = jnp.concatenate([own_w[memory], sent_w[memory]], axis=0)
        gate_up_w = jnp.concatenate([weights[:, :DM], weights[:, DM : 2 * DM]], axis=0)
        out_w = weights[:, 2 * DM :]
        grad_pair = jnp.zeros((2 * hidden, DM), F32)
        grad_out = jnp.zeros((hidden, DM), F32)
        for side in (own, mate):
            key = side[pl.ds(0, tokens), features]
            scaled = side[pl.ds(2 * tokens, tokens), features]
            gate_up = dot_nt(gate_up_w, key)
            gate, up = gate_up[:hidden], gate_up[hidden:]
            sigmoid = jax.nn.sigmoid(gate)
            swish = gate * sigmoid
            slope = sigmoid * (1.0 + gate * (1.0 - sigmoid))
            back = -dot_nt(out_w, scaled)
            pair = jnp.concatenate(
                [(back * up * slope).astype(BF16), (back * swish).astype(BF16)], axis=0
            )
            grad_pair += dot_nn(pair, key)
            grad_out -= dot_nn((swish * up).astype(BF16), scaled)
        found = (grad_pair[:hidden], grad_pair[hidden:], grad_out)
        for part, grad in enumerate(found):
            grad = grad.astype(BF16)
            columns = pl.ds(part * DM, DM)
            if grad_ref.ndim == 3:
                grad_ref[memory, :, columns] = grad
            else:
                blocks, _, rows, _ = grad_ref.shape
                rows //= 2
                for block in range(blocks):
                    for half in range(2):
                        first = half * quarter + block * rows
                        piece = grad[first : first + rows]
                        owned = pl.ds(half * rows, rows)
                        grad_ref[spots[3] ^ block, memory, owned, columns] = piece


def half_grads(spots, blocks, own, mate, own_w, sent_w):
    memories, quarter, width = own_w.shape
    rows = quarter // blocks
    placed = rows % 16 == 0
    shape = (blocks, memories, 2 * rows, width) if placed else (memories, 2 * quarter, width)
    grads = pl.pallas_call(
        grads_kernel,
        out_shape=jax.ShapeDtypeStruct(shape, BF16),
        in_specs=[in_smem()] + in_vmem(4),
        out_specs=in_vmem(1)[0],
        compiler_params=params(),
    )(spots, own, mate, own_w, sent_w)
    if placed:
        return grads
    grads = grads.reshape(memories, 2, blocks, rows, width).transpose(2, 0, 1, 3, 4)
    grads = grads.reshape(blocks, memories, 2 * rows, width)
    return jnp.take(grads, jnp.arange(blocks, dtype=jnp.int32) ^ spots[3], axis=0)


def update_kernel(step_rate, parts, spots, *refs):
    *grads, exact, sent, new_ref = refs
    rows = new_ref.shape[1] // 2
    if exact.shape[1] == rows:
        here = pl.ds(0, rows)
    else:
        here = pl.ds(pl.multiple_of(spots[3] * rows, rows), rows)
    for half, held in enumerate((exact, sent)):
        owned = pl.ds(half * rows, rows)
        total = grads[0][:, owned, :].astype(F32)
        for part in grads[1:]:
            total += part[:, owned, :].astype(F32)
        before = held[:, here, :].astype(F32)
        stepped = before - total * step_rate
        for block in range(3):
            columns = slice(block * DM, (block + 1) * DM)
            old, new = before[..., columns], stepped[..., columns]
            old_norm = jnp.sqrt(jnp.sum(old * old, axis=-1, keepdims=True))
            new_norm = jnp.sqrt(jnp.sum(new * new, axis=-1, keepdims=True) + NORM_EPS)
            new_ref[:, owned, columns] = (new * (old_norm / new_norm)).astype(BF16)


def update_rows(spots, step_rate, grads, exact, sent):
    rows = grads[0].shape[1] // 2
    if rows % 16:
        exact, sent = (
            lax.dynamic_slice_in_dim(held, spots[3] * rows, rows, 1) for held in (exact, sent)
        )
    given = list(grads) + [exact, sent]
    return pl.pallas_call(
        functools.partial(update_kernel, step_rate, len(grads)),
        out_shape=jax.ShapeDtypeStruct(grads[0].shape, BF16),
        in_specs=[in_smem()] + in_vmem(len(given)),
        out_specs=in_vmem(1)[0],
        compiler_params=params(),
    )(spots, *given)


def view_bounds(lengths, own, tokens):
    views = lengths.shape[1]
    down = lax.broadcasted_iota(jnp.int32, (views, views), 0)
    across = lax.broadcasted_iota(jnp.int32, (views, views), 1)
    column = jnp.sum(jnp.where(down == across, lengths[...], 0), axis=1, keepdims=True)
    ends = jnp.sum(jnp.where(down <= across, column, 0), axis=0, keepdims=True)
    spot = own + lax.broadcasted_iota(jnp.int32, (tokens, 1), 0)
    stop = jnp.min(jnp.where(ends > spot, ends, jnp.int32(2**30)), axis=1, keepdims=True)
    start = jnp.max(jnp.where(ends <= spot, ends, 0), axis=1, keepdims=True)
    return start, stop


def inside(base, start, stop):
    place = base + lax.broadcasted_iota(jnp.int32, start.shape, 1)
    return jnp.where((place >= start) & (place < stop), 0.0, MASKED)


SCORE_SCALE = math.log2(math.e) / math.sqrt(HD)


def lanes_wide(column, count):
    return jnp.concatenate([column] * (count // HD), axis=1) if count > HD else column


def summing(values):
    return jnp.concatenate([values, jnp.ones_like(values)], axis=1)


def near_kernel(
    spots, lengths, q_any, own, mate,
    q_ref, last_ref, mixed_ref, peak_ref, sum_ref, bound_ref, sem,
):
    tokens, width = q_ref.shape
    copy = pltpu.make_async_copy(q_any, q_ref, sem)
    copy.start()
    last_ref[...] = own[pl.ds(tokens, tokens), width - DM :]
    bounds = [
        jnp.broadcast_to(bound, (tokens, HD)) for bound in view_bounds(lengths, spots[0], tokens)
    ]
    bound_ref[0], bound_ref[1] = bounds
    copy.wait()
    block_rows = tokens // 4
    for block in range(4):
        rows = slice(block * block_rows, (block + 1) * block_rows)
        start, stop = (lanes_wide(bound[rows], tokens) for bound in bounds)
        shifts = [inside(spots[i], start, stop) for i in range(2)]
        for head in range(width // HD):
            lanes = pl.ds(head * HD, HD)
            query = q_ref[rows, lanes]
            scores = [
                dot_nt(query, side[:tokens, lanes]) + shift
                for shift, side in zip(shifts, (own, mate))
            ]
            peak = jnp.max(jnp.maximum(*scores), axis=1, keepdims=True)
            mixed = sum(
                dot_nn(
                    jnp.exp2((score - peak) * SCORE_SCALE).astype(BF16),
                    summing(side[pl.ds(tokens, tokens), lanes]),
                )
                for score, side in zip(scores, (own, mate))
            )
            mixed_ref[rows, lanes] = mixed[:, :HD]
            peak_ref[head, rows] = jnp.broadcast_to(peak, (block_rows, HD))
            sum_ref[head, rows] = mixed[:, HD:]


def far_kernel(memory, spots, q_ref, far, last, mixed_ref, peak_ref, sum_ref, bound_ref, out_ref):
    tokens, _ = q_ref.shape
    far_k = far.at[pl.ds(2 * memory * tokens, tokens)]
    far_v = last if last is not None else far.at[pl.ds((2 * memory + 1) * tokens, tokens)]
    block_rows = tokens // 4
    for block in range(4):
        rows = slice(block * block_rows, (block + 1) * block_rows)
        start, stop = (lanes_wide(bound_ref[i, rows], tokens) for i in range(2))
        shift = inside(spots[2], start, stop)
        for step in range(DM // HD):
            lanes = pl.ds(step * HD, HD)
            head = memory * (DM // HD) + step
            across = pl.ds(head * HD, HD)
            scores = dot_nt(q_ref[rows, across], far_k[:, lanes]) + shift
            before = peak_ref[head, rows]
            peak = jnp.maximum(before, jnp.max(scores, axis=1, keepdims=True))
            weights = jnp.exp2((scores - lanes_wide(peak, tokens)) * SCORE_SCALE)
            shrink = jnp.exp2((before - peak) * SCORE_SCALE)
            mixed = dot_nn(weights.astype(BF16), summing(far_v[:, lanes]))
            total = sum_ref[head, rows] * shrink + mixed[:, HD:]
            out_ref[rows, lanes] = (mixed_ref[rows, across] * shrink + mixed[:, :HD]) / total


def attend_near(spots, lengths, queries, own, mate):
    tokens, width = queries.shape
    stats = jax.ShapeDtypeStruct((width // HD, tokens, HD), F32)
    bounds = jax.ShapeDtypeStruct((2, tokens, HD), jnp.int32)
    return pl.pallas_call(
        near_kernel,
        out_shape=(
            pltpu.VMEM(queries.shape, BF16),
            pltpu.VMEM((tokens, DM), BF16),
            jax.ShapeDtypeStruct(queries.shape, F32),
            stats,
            stats,
            bounds,
        ),
        in_specs=[in_smem()] + in_vmem(1) + [pl.BlockSpec(memory_space=pltpu.HBM)] + in_vmem(2),
        out_specs=tuple(in_vmem(6)),
        scratch_shapes=[pltpu.SemaphoreType.DMA],
        compiler_params=params(),
    )(spots, lengths, *from_hbm(queries), own, mate)


def attend_far(memory, spots, queries, far, last, near):
    if last is None:

        def body(spots, q_ref, far, *rest):
            far_kernel(memory, spots, q_ref, far, None, *rest)
    else:
        body = functools.partial(far_kernel, memory)
    given = (queries, far) + (() if last is None else (last,)) + tuple(near)
    return pl.pallas_call(
        body,
        out_shape=jax.ShapeDtypeStruct((queries.shape[0], DM), F32),
        in_specs=[in_smem()] + in_vmem(len(given)),
        out_specs=in_vmem(1)[0],
        compiler_params=params(),
    )(spots, *given)


def read_kernel(parts, q_ref, w_ref, *refs):
    before, out_ref = refs[:parts], refs[parts]
    blocks, memories, rows, _ = w_ref.shape
    for memory in range(memories):
        features = pl.ds(memory * DM, DM)
        query = q_ref[:, features]
        weights = w_ref[:, memory].reshape(blocks * rows, 3 * DM)
        gate = dot_nt(query, weights[:, :DM])
        up = dot_nt(query, weights[:, DM : 2 * DM])
        hidden = (gate * jax.nn.sigmoid(gate) * up).astype(BF16)
        total = dot_nn(hidden, weights[:, 2 * DM :])
        if parts > 0:
            total += before[0][:, features] + before[1 + memory][...]
        out_ref[:, features] = total.astype(out_ref.dtype)


def read_half(queries, weights, before, kind):
    return pl.pallas_call(
        functools.partial(read_kernel, len(before)),
        out_shape=jax.ShapeDtypeStruct(queries.shape, kind),
        in_specs=in_vmem(2 + len(before)),
        out_specs=in_vmem(1)[0],
        compiler_params=params(),
    )(queries, weights, *before)


def on_device(queries, keys, values, step_sizes, fast_weights, view_lengths):
    tokens = queries.shape[0]
    memories = queries.shape[1] // DM
    devices = lax.axis_size("tok")
    planes = lax.axis_size("mem")
    chips = devices // CORES
    digits = chip_digits(chips)
    blocks = chips // digits[0]

    def to_core(x):
        return lax.ppermute(x, "tok", [(i, i ^ 1) for i in range(devices)])

    def to_far(x):
        pairs = [
            (i * planes + p, (i + i % 2 * 2 - 1) * planes + p)
            for i in range(1, devices - 1)
            for p in range(planes)
        ]
        for i in (0, devices - 1):
            pairs += [(i * planes + p, i * planes + planes - 1 - p) for p in range(planes)]
        return lax.ppermute(x, ("tok", "mem"), pairs)

    def to_chip(x, flip):
        pairs = [(i, (((i // CORES) ^ flip) * CORES) + i % CORES) for i in range(devices)]
        return lax.ppermute(x, "tok", pairs)

    def to_plane(x):
        return lax.ppermute(x, "mem", [(p, planes - 1 - p) for p in range(planes)])

    spots, own, far, own_w, give_w, exact = stage(
        keys, values, step_sizes, fast_weights, memories, blocks
    )
    sent_w = to_plane(give_w)
    mate = to_core(own)
    far = to_far(far)
    lengths = view_lengths.reshape(1, -1)

    held = half_grads(spots, blocks, own, mate, own_w, sent_w)
    held, lengths = lax.optimization_barrier((held, lengths))
    q, last, *near = attend_near(spots, lengths, queries, own, mate)
    stride = chips
    for place, radix in enumerate(digits[:0:-1]):
        stride //= radix
        held = held.reshape((radix, stride // digits[0]) + held.shape[1:])
        came = [to_chip(held[step], step * stride) for step in range(1, radix)]
        if place == 0:
            came, near = lax.optimization_barrier((came, near))
        held = sum([part.astype(F32) for part in came], held[0].astype(F32)).astype(BF16)
    held = held[0]
    came = [to_chip(held, step) for step in range(1, digits[0])]
    came, last, far = lax.optimization_barrier((came, last, far))
    last = to_far(last)
    all_tokens = tokens * devices
    fresh = update_rows(
        spots, 1.0 / math.sqrt(all_tokens), [held] + came, exact, sent_w
    )

    gathered = fresh[None]
    stride = digits[0]
    for radix in digits[1:]:
        came = [to_chip(gathered, step * stride) for step in range(1, radix)]
        if stride == digits[0]:
            gathered, near = lax.optimization_barrier((gathered, near))
            attended = [
                attend_far(m, spots, q, far, last if m == memories - 1 else None, near)
                for m in range(memories)
            ]
            came, attended = lax.optimization_barrier((came, attended))
        stride *= radix
        gathered = jnp.concatenate([gathered] + came, axis=0)
    mate_w = to_core(gathered)
    partial = read_half(q, gathered, [], F32)
    return read_half(q, mate_w, [partial] + attended, BF16)


def solution(mesh):
    placed = (
        P("tok", "mem"),
        P("tok", "mem"),
        P("tok", "mem"),
        P(None, "tok"),
        P(None, "mem", None),
        P(),
    )
    return jax.shard_map(
        on_device, mesh=mesh, in_specs=placed, out_specs=P("tok", "mem"), check_vma=False
    )
```

```python
import functools
import math

import jax
import jax.numpy as jnp
from jax import lax
from jax.experimental import pallas as pl
from jax.experimental.pallas import tpu as pltpu
from jax.sharding import PartitionSpec as P

DM = 256
HD = 128
CORES = 2
NORM_EPS = 1e-06
VMEM_BYTES = 40 * 2**20
MASKED = -1e30

BF16 = jnp.bfloat16
F32 = jnp.float32


def in_vmem(count):
    return [pl.BlockSpec(memory_space=pltpu.VMEM)] * count


def in_smem():
    return pl.BlockSpec(memory_space=pltpu.SMEM)


def params(limit=VMEM_BYTES):
    return pltpu.CompilerParams(vmem_limit_bytes=limit)


def dot_nt(a, b):
    return lax.dot_general(a, b, (((1,), (1,)), ((), ())), preferred_element_type=F32)


def dot_tn(a, b):
    return lax.dot_general(a, b, (((0,), (0,)), ((), ())), preferred_element_type=F32)


def dot_nn(a, b):
    return jnp.dot(a, b, preferred_element_type=F32)


def chip_digits(chips):
    digits = []
    while chips % 4 == 0:
        digits.append(4)
        chips //= 4
    if chips > 1:
        digits.append(chips)
    return digits[::-1]


def from_hbm(*arrays):
    return [pltpu.with_memory_space_constraint(array, pltpu.HBM) for array in arrays]


def stage_kernel(
    blocks, k_any, v_any, rates_any, weights_any,
    spots, pack_ref, far_ref, w_ref, give_ref, exact_ref,
    held, rates, sems,
):
    spot, plane = lax.axis_index("tok"), lax.axis_index("mem")
    devices, planes = lax.axis_size("tok"), lax.axis_size("mem")
    tokens = pack_ref.shape[0] // 3
    memories, hidden, _ = exact_ref.shape
    core, chip = lax.rem(spot, CORES), lax.div(spot, CORES)
    copies = []

    def bring(source, goal):
        copies.append(pltpu.make_async_copy(source, goal, sems.at[len(copies)]))
        copies[-1].start()

    units = pl.ds(pl.multiple_of(core * hidden, hidden), hidden)
    other = planes - 1 - plane
    bring(weights_any.at[pl.ds(other * memories, memories), units], held)
    bring(weights_any.at[pl.ds(plane * memories, memories), units], exact_ref)
    bring(rates_any, rates)
    bring(v_any, pack_ref.at[pl.ds(tokens, tokens)])
    bring(k_any, pack_ref.at[pl.ds(0, tokens)])
    pieces = [part for m in range(memories) for part in ((k_any, m), (v_any, m))]
    for place, (part, m) in enumerate(pieces[:-1]):
        bring(part.at[:, pl.ds(m * DM, DM)], far_ref.at[pl.ds(place * tokens, tokens)])
    spots[0] = spot * tokens
    spots[1] = (spot ^ 1) * tokens
    spots[2] = jnp.where(core == 0, spot - 1, spot + 1) * tokens
    spots[3] = lax.div(chip, devices // CORES // blocks)
    copies[0].wait()
    for memory in range(memories):
        give_ref[memory] = held[memory].astype(BF16)
    copies[1].wait()
    for memory in range(memories):
        w_ref[memory] = exact_ref[memory].astype(BF16)
    copies[2].wait()
    copies[3].wait()
    turned = jnp.transpose(rates[...])
    for memory in range(memories):
        rate = jnp.zeros((tokens, 1), F32)
        for here in range(planes):
            place = here * memories + memory
            rate = jnp.where(plane == here, turned[:, place : place + 1], rate)
        features = pl.ds(memory * DM, DM)
        value = pack_ref[pl.ds(tokens, tokens), features]
        pack_ref[pl.ds(2 * tokens, tokens), features] = (rate * value.astype(F32)).astype(BF16)
    for copy in copies[4:]:
        copy.wait()


def stage(keys, values, step_sizes, fast_weights, memories, blocks):
    tokens, width = keys.shape
    half = (memories, fast_weights.shape[1] // CORES, 3 * DM)
    return pl.pallas_call(
        functools.partial(stage_kernel, blocks),
        out_shape=(
            jax.ShapeDtypeStruct((8,), jnp.int32),
            pltpu.VMEM((3 * tokens, width), BF16),
            pltpu.VMEM(((2 * memories - 1) * tokens, DM), BF16),
            pltpu.VMEM(half, BF16),
            pltpu.VMEM(half, BF16),
            pltpu.VMEM(half, F32),
        ),
        in_specs=[pl.BlockSpec(memory_space=pltpu.HBM)] * 4,
        out_specs=(in_smem(),) + tuple(in_vmem(5)),
        scratch_shapes=[
            pltpu.VMEM(half, F32),
            pltpu.VMEM(step_sizes.shape, F32),
            pltpu.SemaphoreType.DMA((4 + 2 * memories,)),
        ],
        compiler_params=params(),
    )(*from_hbm(keys, values, step_sizes, fast_weights))


def grads_kernel(spots, own, mate, own_w, sent_w, grad_ref):
    tokens = own.shape[0] // 3
    memories, quarter, _ = own_w.shape
    hidden = 2 * quarter
    for memory in range(memories):
        features = pl.ds(memory * DM, DM)
        weights = jnp.concatenate([own_w[memory], sent_w[memory]], axis=0)
        gate_up_w = jnp.concatenate([weights[:, :DM], weights[:, DM : 2 * DM]], axis=0)
        out_w = weights[:, 2 * DM :]
        grad_pair = jnp.zeros((2 * hidden, DM), F32)
        grad_out = jnp.zeros((hidden, DM), F32)
        for side in (own, mate):
            key = side[pl.ds(0, tokens), features]
            scaled = side[pl.ds(2 * tokens, tokens), features]
            gate_up = dot_nt(gate_up_w, key)
            gate, up = gate_up[:hidden], gate_up[hidden:]
            sigmoid = jax.nn.sigmoid(gate)
            swish = gate * sigmoid
            slope = sigmoid * (1.0 + gate * (1.0 - sigmoid))
            back = -dot_nt(out_w, scaled)
            pair = jnp.concatenate(
                [(back * up * slope).astype(BF16), (back * swish).astype(BF16)], axis=0
            )
            grad_pair += dot_nn(pair, key)
            grad_out -= dot_nn((swish * up).astype(BF16), scaled)
        found = (grad_pair[:hidden], grad_pair[hidden:], grad_out)
        for part, grad in enumerate(found):
            grad = grad.astype(BF16)
            columns = pl.ds(part * DM, DM)
            if grad_ref.ndim == 3:
                grad_ref[memory, :, columns] = grad
            else:
                blocks, _, rows, _ = grad_ref.shape
                rows //= 2
                for block in range(blocks):
                    for half in range(2):
                        first = half * quarter + block * rows
                        piece = grad[first : first + rows]
                        owned = pl.ds(half * rows, rows)
                        grad_ref[spots[3] ^ block, memory, owned, columns] = piece


def half_grads(spots, blocks, own, mate, own_w, sent_w):
    memories, quarter, width = own_w.shape
    rows = quarter // blocks
    placed = rows % 16 == 0
    shape = (blocks, memories, 2 * rows, width) if placed else (memories, 2 * quarter, width)
    grads = pl.pallas_call(
        grads_kernel,
        out_shape=jax.ShapeDtypeStruct(shape, BF16),
        in_specs=[in_smem()] + in_vmem(4),
        out_specs=in_vmem(1)[0],
        compiler_params=params(),
    )(spots, own, mate, own_w, sent_w)
    if placed:
        return grads
    grads = grads.reshape(memories, 2, blocks, rows, width).transpose(2, 0, 1, 3, 4)
    grads = grads.reshape(blocks, memories, 2 * rows, width)
    return jnp.take(grads, jnp.arange(blocks, dtype=jnp.int32) ^ spots[3], axis=0)


def update_kernel(step_rate, parts, spots, *refs):
    *grads, exact, sent, new_ref = refs
    rows = new_ref.shape[1] // 2
    if exact.shape[1] == rows:
        here = pl.ds(0, rows)
    else:
        here = pl.ds(pl.multiple_of(spots[3] * rows, rows), rows)
    for half, held in enumerate((exact, sent)):
        owned = pl.ds(half * rows, rows)
        total = grads[0][:, owned, :].astype(F32)
        for part in grads[1:]:
            total += part[:, owned, :].astype(F32)
        before = held[:, here, :].astype(F32)
        stepped = before - total * step_rate
        for block in range(3):
            columns = slice(block * DM, (block + 1) * DM)
            old, new = before[..., columns], stepped[..., columns]
            old_norm = jnp.sqrt(jnp.sum(old * old, axis=-1, keepdims=True))
            new_norm = jnp.sqrt(jnp.sum(new * new, axis=-1, keepdims=True) + NORM_EPS)
            new_ref[:, owned, columns] = (new * (old_norm / new_norm)).astype(BF16)


def update_rows(spots, step_rate, grads, exact, sent):
    rows = grads[0].shape[1] // 2
    if rows % 16:
        exact, sent = (
            lax.dynamic_slice_in_dim(held, spots[3] * rows, rows, 1) for held in (exact, sent)
        )
    given = list(grads) + [exact, sent]
    return pl.pallas_call(
        functools.partial(update_kernel, step_rate, len(grads)),
        out_shape=jax.ShapeDtypeStruct(grads[0].shape, BF16),
        in_specs=[in_smem()] + in_vmem(len(given)),
        out_specs=in_vmem(1)[0],
        compiler_params=params(),
    )(spots, *given)


def view_bounds(lengths, own, tokens):
    views = lengths.shape[1]
    down = lax.broadcasted_iota(jnp.int32, (views, views), 0)
    across = lax.broadcasted_iota(jnp.int32, (views, views), 1)
    column = jnp.sum(jnp.where(down == across, lengths[...], 0), axis=1, keepdims=True)
    ends = jnp.sum(jnp.where(down <= across, column, 0), axis=0, keepdims=True)
    spot = own + lax.broadcasted_iota(jnp.int32, (tokens, 1), 0)
    stop = jnp.min(jnp.where(ends > spot, ends, jnp.int32(2**30)), axis=1, keepdims=True)
    start = jnp.max(jnp.where(ends <= spot, ends, 0), axis=1, keepdims=True)
    return start, stop


def inside(base, start, stop):
    place = base + lax.broadcasted_iota(jnp.int32, start.shape, 1)
    return jnp.where((place >= start) & (place < stop), 0.0, MASKED)


SCORE_SCALE = math.log2(math.e) / math.sqrt(HD)


def lanes_wide(column, count):
    return jnp.concatenate([column] * (count // HD), axis=1) if count > HD else column


def summing(values):
    return jnp.concatenate([values, jnp.ones_like(values)], axis=1)


def near_kernel(
    spots, lengths, q_any, own, mate,
    q_ref, last_ref, mixed_ref, peak_ref, sum_ref, bound_ref, sem,
):
    tokens, width = q_ref.shape
    copy = pltpu.make_async_copy(q_any, q_ref, sem)
    copy.start()
    last_ref[...] = own[pl.ds(tokens, tokens), width - DM :]
    bounds = [
        jnp.broadcast_to(bound, (tokens, HD)) for bound in view_bounds(lengths, spots[0], tokens)
    ]
    bound_ref[0], bound_ref[1] = bounds
    copy.wait()
    block_rows = tokens // 4
    for block in range(4):
        rows = slice(block * block_rows, (block + 1) * block_rows)
        start, stop = (lanes_wide(bound[rows], tokens) for bound in bounds)
        shifts = [inside(spots[i], start, stop) for i in range(2)]
        for head in range(width // HD):
            lanes = pl.ds(head * HD, HD)
            query = q_ref[rows, lanes]
            scores = [
                dot_nt(query, side[:tokens, lanes]) + shift
                for shift, side in zip(shifts, (own, mate))
            ]
            peak = jnp.max(jnp.maximum(*scores), axis=1, keepdims=True)
            mixed = sum(
                dot_nn(
                    jnp.exp2((score - peak) * SCORE_SCALE).astype(BF16),
                    summing(side[pl.ds(tokens, tokens), lanes]),
                )
                for score, side in zip(scores, (own, mate))
            )
            mixed_ref[rows, lanes] = mixed[:, :HD]
            peak_ref[head, rows] = jnp.broadcast_to(peak, (block_rows, HD))
            sum_ref[head, rows] = mixed[:, HD:]


def far_kernel(memory, spots, q_ref, far, last, mixed_ref, peak_ref, sum_ref, bound_ref, out_ref):
    tokens, _ = q_ref.shape
    far_k = far.at[pl.ds(2 * memory * tokens, tokens)]
    far_v = last if last is not None else far.at[pl.ds((2 * memory + 1) * tokens, tokens)]
    block_rows = tokens // 4
    for block in range(4):
        rows = slice(block * block_rows, (block + 1) * block_rows)
        start, stop = (lanes_wide(bound_ref[i, rows], tokens) for i in range(2))
        shift = inside(spots[2], start, stop)
        for step in range(DM // HD):
            lanes = pl.ds(step * HD, HD)
            head = memory * (DM // HD) + step
            across = pl.ds(head * HD, HD)
            scores = dot_nt(q_ref[rows, across], far_k[:, lanes]) + shift
            before = peak_ref[head, rows]
            peak = jnp.maximum(before, jnp.max(scores, axis=1, keepdims=True))
            weights = jnp.exp2((scores - lanes_wide(peak, tokens)) * SCORE_SCALE)
            shrink = jnp.exp2((before - peak) * SCORE_SCALE)
            mixed = dot_nn(weights.astype(BF16), summing(far_v[:, lanes]))
            total = sum_ref[head, rows] * shrink + mixed[:, HD:]
            out_ref[rows, lanes] = (mixed_ref[rows, across] * shrink + mixed[:, :HD]) / total


def attend_near(spots, lengths, queries, own, mate):
    tokens, width = queries.shape
    stats = jax.ShapeDtypeStruct((width // HD, tokens, HD), F32)
    bounds = jax.ShapeDtypeStruct((2, tokens, HD), jnp.int32)
    return pl.pallas_call(
        near_kernel,
        out_shape=(
            pltpu.VMEM(queries.shape, BF16),
            pltpu.VMEM((tokens, DM), BF16),
            jax.ShapeDtypeStruct(queries.shape, F32),
            stats,
            stats,
            bounds,
        ),
        in_specs=[in_smem()] + in_vmem(1) + [pl.BlockSpec(memory_space=pltpu.HBM)] + in_vmem(2),
        out_specs=tuple(in_vmem(6)),
        scratch_shapes=[pltpu.SemaphoreType.DMA],
        compiler_params=params(),
    )(spots, lengths, *from_hbm(queries), own, mate)


def attend_far(memory, spots, queries, far, last, near):
    if last is None:

        def body(spots, q_ref, far, *rest):
            far_kernel(memory, spots, q_ref, far, None, *rest)
    else:
        body = functools.partial(far_kernel, memory)
    given = (queries, far) + (() if last is None else (last,)) + tuple(near)
    return pl.pallas_call(
        body,
        out_shape=jax.ShapeDtypeStruct((queries.shape[0], DM), F32),
        in_specs=[in_smem()] + in_vmem(len(given)),
        out_specs=in_vmem(1)[0],
        compiler_params=params(),
    )(spots, *given)


def read_kernel(q_ref, w_ref, out_ref):
    blocks, memories, rows, width = w_ref.shape
    for memory in range(memories):
        features = pl.ds(memory * DM, DM)
        out_ref[:, features] = read_rows(q_ref[:, features], w_ref[:, memory])


def read_rows(query, weights):
    held = weights.reshape(weights.shape[0] * weights.shape[1], weights.shape[2])
    units = held.shape[0]
    gate_up = dot_nt(query, jnp.concatenate([held[:, :DM], held[:, DM : 2 * DM]], axis=0))
    gate, up = gate_up[:, :units], gate_up[:, units:]
    hidden = (gate * jax.nn.sigmoid(gate) * up).astype(BF16)
    return dot_nn(hidden, held[:, 2 * DM :])


def last_kernel(q_ref, w_ref, before, *refs):
    *attended, out_any, result, sems = refs
    copies = []
    for memory in range(w_ref.shape[1]):
        features = pl.ds(memory * DM, DM)
        total = read_rows(q_ref[:, features], w_ref[:, memory])
        total += before[:, features] + attended[memory][...]
        result[:, features] = total.astype(BF16)
        done, goal = result.at[:, features], out_any.at[:, features]
        copies.append(pltpu.make_async_copy(done, goal, sems.at[memory]))
        copies[-1].start()
    for copy in copies:
        copy.wait()


def read_first(queries, weights):
    return pl.pallas_call(
        read_kernel,
        out_shape=jax.ShapeDtypeStruct(queries.shape, F32),
        in_specs=in_vmem(2),
        out_specs=in_vmem(1)[0],
        compiler_params=params(),
    )(queries, weights)


def read_last(queries, weights, before, attended):
    return pl.pallas_call(
        last_kernel,
        out_shape=jax.ShapeDtypeStruct(queries.shape, BF16),
        in_specs=in_vmem(3 + len(attended)),
        out_specs=pl.BlockSpec(memory_space=pltpu.HBM),
        scratch_shapes=[pltpu.VMEM(queries.shape, BF16), pltpu.SemaphoreType.DMA((len(attended),))],
        compiler_params=params(),
    )(queries, weights, before, *attended)


def on_device(queries, keys, values, step_sizes, fast_weights, view_lengths):
    tokens = queries.shape[0]
    memories = queries.shape[1] // DM
    devices = lax.axis_size("tok")
    planes = lax.axis_size("mem")
    chips = devices // CORES
    digits = chip_digits(chips)
    blocks = chips // digits[0]

    def to_core(x):
        return lax.ppermute(x, "tok", [(i, i ^ 1) for i in range(devices)])

    def to_far(x):
        pairs = [
            (i * planes + p, (i + i % 2 * 2 - 1) * planes + p)
            for i in range(1, devices - 1)
            for p in range(planes)
        ]
        for i in (0, devices - 1):
            pairs += [(i * planes + p, i * planes + planes - 1 - p) for p in range(planes)]
        return lax.ppermute(x, ("tok", "mem"), pairs)

    def to_chip(x, flip):
        pairs = [(i, (((i // CORES) ^ flip) * CORES) + i % CORES) for i in range(devices)]
        return lax.ppermute(x, "tok", pairs)

    def to_plane(x):
        return lax.ppermute(x, "mem", [(p, planes - 1 - p) for p in range(planes)])

    spots, own, far, own_w, give_w, exact = stage(
        keys, values, step_sizes, fast_weights, memories, blocks
    )
    sent_w = to_plane(give_w)
    mate = to_core(own)
    far = to_far(far)
    lengths = view_lengths.reshape(1, -1)

    held = half_grads(spots, blocks, own, mate, own_w, sent_w)
    held, lengths = lax.optimization_barrier((held, lengths))
    q, last, *near = attend_near(spots, lengths, queries, own, mate)
    stride = chips
    for place, radix in enumerate(digits[:0:-1]):
        stride //= radix
        held = held.reshape((radix, stride // digits[0]) + held.shape[1:])
        came = [to_chip(held[step], step * stride) for step in range(1, radix)]
        if place == 0:
            came, near = lax.optimization_barrier((came, near))
        held = sum([part.astype(F32) for part in came], held[0].astype(F32)).astype(BF16)
    held = held[0]
    came = [to_chip(held, step) for step in range(1, digits[0])]
    came, last, far = lax.optimization_barrier((came, last, far))
    last = to_far(last)
    all_tokens = tokens * devices
    fresh = update_rows(
        spots, 1.0 / math.sqrt(all_tokens), [held] + came, exact, sent_w
    )

    gathered = fresh[None]
    stride = digits[0]
    for radix in digits[1:]:
        came = [to_chip(gathered, step * stride) for step in range(1, radix)]
        if stride == digits[0]:
            gathered, near = lax.optimization_barrier((gathered, near))
            attended = [
                attend_far(m, spots, q, far, last if m == memories - 1 else None, near)
                for m in range(memories)
            ]
            came, attended = lax.optimization_barrier((came, attended))
        stride *= radix
        gathered = jnp.concatenate([gathered] + came, axis=0)
    mate_w = to_core(gathered)
    partial = read_first(q, gathered)
    return read_last(q, mate_w, partial, attended)


def solution(mesh):
    placed = (
        P("tok", "mem"),
        P("tok", "mem"),
        P("tok", "mem"),
        P(None, "tok"),
        P(None, "mem", None),
        P(),
    )
    return jax.shard_map(
        on_device, mesh=mesh, in_specs=placed, out_specs=P("tok", "mem"), check_vma=False
    )
```

```python
import functools
import math

import jax
import jax.numpy as jnp
from jax import lax
from jax.experimental import pallas as pl
from jax.experimental.pallas import tpu as pltpu
from jax.sharding import PartitionSpec as P

DM = 256
HD = 128
CORES = 2
NORM_EPS = 1e-06
VMEM_BYTES = 40 * 2**20
MASKED = -1e30

BF16 = jnp.bfloat16
F32 = jnp.float32


def in_vmem(count):
    return [pl.BlockSpec(memory_space=pltpu.VMEM)] * count


def in_smem():
    return pl.BlockSpec(memory_space=pltpu.SMEM)


def params(limit=VMEM_BYTES):
    return pltpu.CompilerParams(vmem_limit_bytes=limit)


def dot_nt(a, b):
    return lax.dot_general(a, b, (((1,), (1,)), ((), ())), preferred_element_type=F32)


def dot_tn(a, b):
    return lax.dot_general(a, b, (((0,), (0,)), ((), ())), preferred_element_type=F32)


def dot_nn(a, b):
    return jnp.dot(a, b, preferred_element_type=F32)


def chip_digits(chips):
    digits = []
    while chips % 4 == 0:
        digits.append(4)
        chips //= 4
    if chips > 1:
        digits.append(chips)
    return digits[::-1]


def from_hbm(*arrays):
    return [pltpu.with_memory_space_constraint(array, pltpu.HBM) for array in arrays]


def stage_kernel(
    blocks, k_any, v_any, rates_any, weights_any,
    spots, pack_ref, far_ref, w_ref, give_ref, exact_ref,
    held, rates, sems,
):
    spot, plane = lax.axis_index("tok"), lax.axis_index("mem")
    devices, planes = lax.axis_size("tok"), lax.axis_size("mem")
    tokens = pack_ref.shape[0] // 3
    memories, hidden, _ = exact_ref.shape
    core, chip = lax.rem(spot, CORES), lax.div(spot, CORES)
    copies = []

    def bring(source, goal):
        copies.append(pltpu.make_async_copy(source, goal, sems.at[len(copies)]))
        copies[-1].start()

    units = pl.ds(pl.multiple_of(core * hidden, hidden), hidden)
    other = planes - 1 - plane
    bring(weights_any.at[pl.ds(other * memories, memories), units], held)
    bring(weights_any.at[pl.ds(plane * memories, memories), units], exact_ref)
    bring(rates_any, rates)
    bring(v_any, pack_ref.at[pl.ds(tokens, tokens)])
    bring(k_any, pack_ref.at[pl.ds(0, tokens)])
    pieces = [part for m in range(memories) for part in ((k_any, m), (v_any, m))]
    for place, (part, m) in enumerate(pieces[:-1]):
        bring(part.at[:, pl.ds(m * DM, DM)], far_ref.at[pl.ds(place * tokens, tokens)])
    spots[0] = spot * tokens
    spots[1] = (spot ^ 1) * tokens
    spots[2] = jnp.where(core == 0, spot - 1, spot + 1) * tokens
    spots[3] = lax.div(chip, devices // CORES // blocks)
    copies[0].wait()
    for memory in range(memories):
        give_ref[memory] = held[memory].astype(BF16)
    copies[1].wait()
    for memory in range(memories):
        w_ref[memory] = exact_ref[memory].astype(BF16)
    copies[2].wait()
    copies[3].wait()
    turned = jnp.transpose(rates[...])
    for memory in range(memories):
        rate = jnp.zeros((tokens, 1), F32)
        for here in range(planes):
            place = here * memories + memory
            rate = jnp.where(plane == here, turned[:, place : place + 1], rate)
        features = pl.ds(memory * DM, DM)
        value = pack_ref[pl.ds(tokens, tokens), features]
        pack_ref[pl.ds(2 * tokens, tokens), features] = (rate * value.astype(F32)).astype(BF16)
    for copy in copies[4:]:
        copy.wait()


def stage(keys, values, step_sizes, fast_weights, memories, blocks):
    tokens, width = keys.shape
    half = (memories, fast_weights.shape[1] // CORES, 3 * DM)
    return pl.pallas_call(
        functools.partial(stage_kernel, blocks),
        out_shape=(
            jax.ShapeDtypeStruct((8,), jnp.int32),
            pltpu.VMEM((3 * tokens, width), BF16),
            pltpu.VMEM(((2 * memories - 1) * tokens, DM), BF16),
            pltpu.VMEM(half, BF16),
            pltpu.VMEM(half, BF16),
            pltpu.VMEM(half, F32),
        ),
        in_specs=[pl.BlockSpec(memory_space=pltpu.HBM)] * 4,
        out_specs=(in_smem(),) + tuple(in_vmem(5)),
        scratch_shapes=[
            pltpu.VMEM(half, F32),
            pltpu.VMEM(step_sizes.shape, F32),
            pltpu.SemaphoreType.DMA((4 + 2 * memories,)),
        ],
        compiler_params=params(),
    )(*from_hbm(keys, values, step_sizes, fast_weights))


def grads_kernel(spots, own, mate, own_w, sent_w, grad_ref):
    tokens = own.shape[0] // 3
    memories, quarter, _ = own_w.shape
    hidden = 2 * quarter
    for memory in range(memories):
        features = pl.ds(memory * DM, DM)
        weights = jnp.concatenate([own_w[memory], sent_w[memory]], axis=0)
        gate_up_w = jnp.concatenate([weights[:, :DM], weights[:, DM : 2 * DM]], axis=0)
        out_w = weights[:, 2 * DM :]
        grad_pair = jnp.zeros((2 * hidden, DM), F32)
        grad_out = jnp.zeros((hidden, DM), F32)
        for side in (own, mate):
            key = side[pl.ds(0, tokens), features]
            scaled = side[pl.ds(2 * tokens, tokens), features]
            gate_up = dot_nt(gate_up_w, key)
            gate, up = gate_up[:hidden], gate_up[hidden:]
            sigmoid = jax.nn.sigmoid(gate)
            swish = gate * sigmoid
            slope = sigmoid * (1.0 + gate * (1.0 - sigmoid))
            back = -dot_nt(out_w, scaled)
            pair = jnp.concatenate(
                [(back * up * slope).astype(BF16), (back * swish).astype(BF16)], axis=0
            )
            grad_pair += dot_nn(pair, key)
            grad_out -= dot_nn((swish * up).astype(BF16), scaled)
        found = (grad_pair[:hidden], grad_pair[hidden:], grad_out)
        for part, grad in enumerate(found):
            grad = grad.astype(BF16)
            columns = pl.ds(part * DM, DM)
            if grad_ref.ndim == 3:
                grad_ref[memory, :, columns] = grad
            else:
                blocks, _, rows, _ = grad_ref.shape
                rows //= 2
                for block in range(blocks):
                    for half in range(2):
                        first = half * quarter + block * rows
                        piece = grad[first : first + rows]
                        owned = pl.ds(half * rows, rows)
                        grad_ref[spots[3] ^ block, memory, owned, columns] = piece


def half_grads(spots, blocks, own, mate, own_w, sent_w):
    memories, quarter, width = own_w.shape
    rows = quarter // blocks
    placed = rows % 16 == 0
    shape = (blocks, memories, 2 * rows, width) if placed else (memories, 2 * quarter, width)
    grads = pl.pallas_call(
        grads_kernel,
        out_shape=jax.ShapeDtypeStruct(shape, BF16),
        in_specs=[in_smem()] + in_vmem(4),
        out_specs=in_vmem(1)[0],
        compiler_params=params(),
    )(spots, own, mate, own_w, sent_w)
    if placed:
        return grads
    grads = grads.reshape(memories, 2, blocks, rows, width).transpose(2, 0, 1, 3, 4)
    grads = grads.reshape(blocks, memories, 2 * rows, width)
    return jnp.take(grads, jnp.arange(blocks, dtype=jnp.int32) ^ spots[3], axis=0)


def update_kernel(step_rate, parts, spots, *refs):
    *grads, exact, sent, new_ref = refs
    rows = new_ref.shape[1] // 2
    if exact.shape[1] == rows:
        here = pl.ds(0, rows)
    else:
        here = pl.ds(pl.multiple_of(spots[3] * rows, rows), rows)
    for half, held in enumerate((exact, sent)):
        owned = pl.ds(half * rows, rows)
        total = grads[0][:, owned, :].astype(F32)
        for part in grads[1:]:
            total += part[:, owned, :].astype(F32)
        before = held[:, here, :].astype(F32)
        stepped = before - total * step_rate
        for block in range(3):
            columns = slice(block * DM, (block + 1) * DM)
            old, new = before[..., columns], stepped[..., columns]
            old_norm = jnp.sqrt(jnp.sum(old * old, axis=-1, keepdims=True))
            new_norm = jnp.sqrt(jnp.sum(new * new, axis=-1, keepdims=True) + NORM_EPS)
            new_ref[:, owned, columns] = (new * (old_norm / new_norm)).astype(BF16)


def update_rows(spots, step_rate, grads, exact, sent):
    rows = grads[0].shape[1] // 2
    if rows % 16:
        exact, sent = (
            lax.dynamic_slice_in_dim(held, spots[3] * rows, rows, 1) for held in (exact, sent)
        )
    given = list(grads) + [exact, sent]
    return pl.pallas_call(
        functools.partial(update_kernel, step_rate, len(grads)),
        out_shape=jax.ShapeDtypeStruct(grads[0].shape, BF16),
        in_specs=[in_smem()] + in_vmem(len(given)),
        out_specs=in_vmem(1)[0],
        compiler_params=params(),
    )(spots, *given)


def view_bounds(lengths, own, tokens):
    views = lengths.shape[1]
    down = lax.broadcasted_iota(jnp.int32, (views, views), 0)
    across = lax.broadcasted_iota(jnp.int32, (views, views), 1)
    column = jnp.sum(jnp.where(down == across, lengths[...], 0), axis=1, keepdims=True)
    ends = jnp.sum(jnp.where(down <= across, column, 0), axis=0, keepdims=True)
    spot = own + lax.broadcasted_iota(jnp.int32, (tokens, 1), 0)
    stop = jnp.min(jnp.where(ends > spot, ends, jnp.int32(2**30)), axis=1, keepdims=True)
    start = jnp.max(jnp.where(ends <= spot, ends, 0), axis=1, keepdims=True)
    return start, stop


def inside(base, start, stop):
    place = base + lax.broadcasted_iota(jnp.int32, start.shape, 1)
    return jnp.where((place >= start) & (place < stop), 0.0, MASKED)


SCORE_SCALE = math.log2(math.e) / math.sqrt(HD)


def lanes_wide(column, count):
    return jnp.concatenate([column] * (count // HD), axis=1) if count > HD else column


def summing(values):
    return jnp.concatenate([values, jnp.ones_like(values)], axis=1)


def near_kernel(
    spots, lengths, q_any, own, mate,
    q_ref, last_ref, mixed_ref, peak_ref, sum_ref, bound_ref, sem,
):
    tokens, width = q_ref.shape
    copy = pltpu.make_async_copy(q_any, q_ref, sem)
    copy.start()
    last_ref[...] = own[pl.ds(tokens, tokens), width - DM :]
    bounds = [
        jnp.broadcast_to(bound, (tokens, HD)) for bound in view_bounds(lengths, spots[0], tokens)
    ]
    bound_ref[0], bound_ref[1] = bounds
    copy.wait()
    block_rows = tokens // 4
    for block in range(4):
        rows = slice(block * block_rows, (block + 1) * block_rows)
        start, stop = (lanes_wide(bound[rows], tokens) for bound in bounds)
        shifts = [inside(spots[i], start, stop) for i in range(2)]
        for head in range(width // HD):
            lanes = pl.ds(head * HD, HD)
            query = q_ref[rows, lanes]
            scores = [
                dot_nt(query, side[:tokens, lanes]) + shift
                for shift, side in zip(shifts, (own, mate))
            ]
            peak = jnp.max(jnp.maximum(*scores), axis=1, keepdims=True)
            mixed = sum(
                dot_nn(
                    jnp.exp2((score - peak) * SCORE_SCALE).astype(BF16),
                    summing(side[pl.ds(tokens, tokens), lanes]),
                )
                for score, side in zip(scores, (own, mate))
            )
            mixed_ref[rows, lanes] = mixed[:, :HD]
            peak_ref[head, rows] = jnp.broadcast_to(peak, (block_rows, HD))
            sum_ref[head, rows] = mixed[:, HD:]


def far_kernel(memory, spots, q_ref, far, last, mixed_ref, peak_ref, sum_ref, bound_ref, out_ref):
    tokens, _ = q_ref.shape
    far_k = far.at[pl.ds(2 * memory * tokens, tokens)]
    far_v = last if last is not None else far.at[pl.ds((2 * memory + 1) * tokens, tokens)]
    block_rows = tokens // 4
    for block in range(4):
        rows = slice(block * block_rows, (block + 1) * block_rows)
        start, stop = (lanes_wide(bound_ref[i, rows], tokens) for i in range(2))
        shift = inside(spots[2], start, stop)
        for step in range(DM // HD):
            lanes = pl.ds(step * HD, HD)
            head = memory * (DM // HD) + step
            across = pl.ds(head * HD, HD)
            scores = dot_nt(q_ref[rows, across], far_k[:, lanes]) + shift
            before = peak_ref[head, rows]
            peak = jnp.maximum(before, jnp.max(scores, axis=1, keepdims=True))
            weights = jnp.exp2((scores - lanes_wide(peak, tokens)) * SCORE_SCALE)
            shrink = jnp.exp2((before - peak) * SCORE_SCALE)
            mixed = dot_nn(weights.astype(BF16), summing(far_v[:, lanes]))
            total = sum_ref[head, rows] * shrink + mixed[:, HD:]
            out_ref[rows, lanes] = (mixed_ref[rows, across] * shrink + mixed[:, :HD]) / total


def attend_near(spots, lengths, queries, own, mate):
    tokens, width = queries.shape
    stats = jax.ShapeDtypeStruct((width // HD, tokens, HD), F32)
    bounds = jax.ShapeDtypeStruct((2, tokens, HD), jnp.int32)
    return pl.pallas_call(
        near_kernel,
        out_shape=(
            pltpu.VMEM(queries.shape, BF16),
            pltpu.VMEM((tokens, DM), BF16),
            jax.ShapeDtypeStruct(queries.shape, F32),
            stats,
            stats,
            bounds,
        ),
        in_specs=[in_smem()] + in_vmem(1) + [pl.BlockSpec(memory_space=pltpu.HBM)] + in_vmem(2),
        out_specs=tuple(in_vmem(6)),
        scratch_shapes=[pltpu.SemaphoreType.DMA],
        compiler_params=params(),
    )(spots, lengths, *from_hbm(queries), own, mate)


def attend_far(memory, spots, queries, far, last, near):
    if last is None:

        def body(spots, q_ref, far, *rest):
            far_kernel(memory, spots, q_ref, far, None, *rest)
    else:
        body = functools.partial(far_kernel, memory)
    given = (queries, far) + (() if last is None else (last,)) + tuple(near)
    return pl.pallas_call(
        body,
        out_shape=jax.ShapeDtypeStruct((queries.shape[0], DM), F32),
        in_specs=[in_smem()] + in_vmem(len(given)),
        out_specs=in_vmem(1)[0],
        compiler_params=params(),
    )(spots, *given)


def read_kernel(q_ref, w_ref, out_ref):
    blocks, memories, rows, width = w_ref.shape
    for memory in range(memories):
        features = pl.ds(memory * DM, DM)
        out_ref[:, features] = read_rows(q_ref[:, features], w_ref[:, memory])


def read_rows(query, weights):
    held = weights.reshape(weights.shape[0] * weights.shape[1], weights.shape[2])
    units = held.shape[0]
    gate_up = dot_nt(query, jnp.concatenate([held[:, :DM], held[:, DM : 2 * DM]], axis=0))
    gate, up = gate_up[:, :units], gate_up[:, units:]
    hidden = (gate * jax.nn.sigmoid(gate) * up).astype(BF16)
    return dot_nn(hidden, held[:, 2 * DM :])


def last_kernel(q_ref, w_ref, before, *refs):
    *attended, out_any, result, sems = refs
    copies = []
    for memory in range(w_ref.shape[1]):
        features = pl.ds(memory * DM, DM)
        total = read_rows(q_ref[:, features], w_ref[:, memory])
        total += before[:, features] + attended[memory][...]
        result[:, features] = total.astype(BF16)
        done, goal = result.at[:, features], out_any.at[:, features]
        copies.append(pltpu.make_async_copy(done, goal, sems.at[memory]))
        copies[-1].start()
    for copy in copies:
        copy.wait()


def read_first(queries, weights):
    return pl.pallas_call(
        read_kernel,
        out_shape=jax.ShapeDtypeStruct(queries.shape, F32),
        in_specs=in_vmem(2),
        out_specs=in_vmem(1)[0],
        compiler_params=params(),
    )(queries, weights)


def read_last(queries, weights, before, attended):
    return pl.pallas_call(
        last_kernel,
        out_shape=jax.ShapeDtypeStruct(queries.shape, BF16),
        in_specs=in_vmem(3 + len(attended)),
        out_specs=pl.BlockSpec(memory_space=pltpu.HBM),
        scratch_shapes=[pltpu.VMEM(queries.shape, BF16), pltpu.SemaphoreType.DMA((len(attended),))],
        compiler_params=params(),
    )(queries, weights, before, *attended)


def on_device(queries, keys, values, step_sizes, fast_weights, view_lengths):
    tokens = queries.shape[0]
    memories = queries.shape[1] // DM
    devices = lax.axis_size("tok")
    planes = lax.axis_size("mem")
    chips = devices // CORES
    digits = chip_digits(chips)
    blocks = chips // digits[0]

    def to_core(x):
        return lax.ppermute(x, "tok", [(i, i ^ 1) for i in range(devices)])

    def to_far(x):
        pairs = [
            (i * planes + p, (i + i % 2 * 2 - 1) * planes + p)
            for i in range(1, devices - 1)
            for p in range(planes)
        ]
        for i in (0, devices - 1):
            pairs += [(i * planes + p, i * planes + planes - 1 - p) for p in range(planes)]
        return lax.ppermute(x, ("tok", "mem"), pairs)

    def to_chip(x, flip):
        pairs = [(i, (((i // CORES) ^ flip) * CORES) + i % CORES) for i in range(devices)]
        return lax.ppermute(x, "tok", pairs)

    def to_plane(x):
        return lax.ppermute(x, "mem", [(p, planes - 1 - p) for p in range(planes)])

    spots, own, far, own_w, give_w, exact = stage(
        keys, values, step_sizes, fast_weights, memories, blocks
    )
    sent_w = to_plane(give_w)
    mate = to_core(own)
    far = to_far(far)
    lengths = view_lengths.reshape(1, -1)

    held = half_grads(spots, blocks, own, mate, own_w, sent_w)
    held, lengths = lax.optimization_barrier((held, lengths))
    q, last, *near = attend_near(spots, lengths, queries, own, mate)
    stride = chips
    for place, radix in enumerate(digits[:0:-1]):
        stride //= radix
        held = held.reshape((radix, stride // digits[0]) + held.shape[1:])
        came = [to_chip(held[step], step * stride) for step in sorted(range(1, radix), key=lambda step: (step % 2, step))]
        if place == 0:
            came, near = lax.optimization_barrier((came, near))
        held = sum([part.astype(F32) for part in came], held[0].astype(F32)).astype(BF16)
    held = held[0]
    came = [to_chip(held, step) for step in range(1, digits[0])]
    came, last, far = lax.optimization_barrier((came, last, far))
    last = to_far(last)
    all_tokens = tokens * devices
    fresh = update_rows(
        spots, 1.0 / math.sqrt(all_tokens), [held] + came, exact, sent_w
    )

    gathered = fresh[None]
    stride = digits[0]
    for radix in digits[1:]:
        came = [to_chip(gathered, step * stride) for step in sorted(range(1, radix), key=lambda step: (step % 2, step))]
        if stride == digits[0]:
            gathered, near = lax.optimization_barrier((gathered, near))
            attended = [
                attend_far(m, spots, q, far, last if m == memories - 1 else None, near)
                for m in range(memories)
            ]
            came, attended = lax.optimization_barrier((came, attended))
        stride *= radix
        gathered = jnp.concatenate([gathered] + came, axis=0)
    mate_w = to_core(gathered)
    partial = read_first(q, gathered)
    return read_last(q, mate_w, partial, attended)


def solution(mesh):
    placed = (
        P("tok", "mem"),
        P("tok", "mem"),
        P("tok", "mem"),
        P(None, "tok"),
        P(None, "mem", None),
        P(),
    )
    return jax.shard_map(
        on_device, mesh=mesh, in_specs=placed, out_specs=P("tok", "mem"), check_vma=False
    )
```
